128 devices in a mesh: seq: 16 (over x, y), tp: 8 (over z, core).
Axes of the slice: x: 4, y: 4, z: 4, core: 2. Of those that a mesh axis runs over, the one named last changes fastest.
Arguments:
- x_in: bfloat16 [16, 4096, 8192], P('tp', 'seq'), may hold values from -6 to 6
- dt_raw: bfloat16 [16, 4096, 128], P('tp', 'seq'), may hold values from -4 to 4
- bc_in: bfloat16 [16, 4096, 32], P('tp', 'seq'), may hold values from -1.1953125 to 1.1953125
- decay_rate: float32 [128], replicated, may hold values from 2.4414063e-05 to 0.1
- skip_gain: float32 [128], replicated, may hold values from 0.5 to 1.5
- kv_pre: bfloat16 [16, 4096, 2048], P('tp', 'seq'), may hold values from -8 to 8
- lengths: int32 [16], replicated, may hold values from 256 to 4096, as said below
- group_of: int32 [16], replicated, may hold values from 0 to 15, each once
- slot_of: int32 [16, 16], replicated, may hold values from 0 to 15, each once within a row
- dec_x: bfloat16 [16, 4, 8192], P('seq', None, 'tp'), may hold values from -6 to 6
- dec_dt: bfloat16 [16, 4, 128], P('seq', None, 'tp'), may hold values from -4 to 4
- dec_bc: bfloat16 [16, 4, 32], P('seq'), may hold values from -1.1953125 to 1.1953125
- dec_z: bfloat16 [16, 4, 8192], P('seq', None, 'tp'), may hold values from -6 to 6
- norm_gain: bfloat16 [8192], P('tp'), may hold values from 0.5 to 1.5
- dec_q: bfloat16 [16, 4, 8192], P('seq', None, 'tp'), may hold values from -8 to 8
- dec_kv: bfloat16 [16, 4, 2048], P('seq', None, 'tp'), may hold values from -6 to 6
Outputs:
- y_pre: bfloat16 [16, 4096, 8192], P('tp', 'seq')
- kv_pool: bfloat16 [16, 4096, 2048], P('seq', None, 'tp')
- dec_mamba: bfloat16 [16, 4, 8192], P('seq', None, 'tp')
- dec_state: float32 [16, 16, 8192], P('seq', None, 'tp')
- dec_attn: bfloat16 [16, 4, 8192], P('seq', None, 'tp')
The draws below stay inside these ranges and needn't reach their ends.
Inputs may be any that keep to these rules, and one draw needn't show every extreme that they name: `lengths`: every length is a multiple of 256; some prompt has length 4096. `group_of`: every decode group serves exactly one prompt. `slot_of`: each row is a permutation of the 16 slots.
All inputs are finite; a program needn't handle non-finite values.
Results may differ from the reference program's by a relative error of at most 0.005.
Values may be sent and summed in bfloat16 or wider, within the bound.
No kernel may reach another device: no remote copies, remote signals or barrier semaphores. Data moves between devices by JAX's collectives and lax.ppermute only.
A program may use at most 128 MiB of HBM per device.

```python
import math
import jax
import jax.numpy as jnp
from jax import lax

EW = 8192
HP = 64
HEADS_M = 128
NS = 16
QH = 64
KVH = 8
HD = 128
BLK = 256
PAGE = 256
STEPS = 4
LENGTH = 4096
REQUESTS = 16
PAGES = 16


def draw_lengths(key, part):
    key = jax.random.fold_in(key, 11)
    key_pages, key_longest = jax.random.split(key)
    pages = jax.random.randint(key_pages, (REQUESTS,), 1, PAGES + 1)
    longest = jax.random.randint(key_longest, (), 0, REQUESTS)
    pages = jnp.where(jnp.arange(REQUESTS) == longest, PAGES, pages)
    return (pages * PAGE).astype(jnp.int32)


def draw_kv_pre(key, part):
    key = jax.random.fold_in(key, 23)
    key_normal = jax.random.fold_in(key, 0)
    entries = jnp.clip(jax.random.normal(key_normal, (REQUESTS, LENGTH, KVH, 2, HD), jnp.float32), -6.0, 6.0)
    return entries.reshape(REQUESTS, LENGTH, KVH * 2 * HD).astype(jnp.bfloat16)


def draw_dec_q(key, part):
    key = jax.random.fold_in(key, 29)
    key_normal = jax.random.fold_in(key, 0)
    entries = jnp.clip(jax.random.normal(key_normal, (REQUESTS, STEPS, QH, HD), jnp.float32), -6.0, 6.0)
    return entries.reshape(REQUESTS, STEPS, QH * HD).astype(jnp.bfloat16)


def block_scale(stream_key, extent, cuts, low, high):
    loudness = 1.0
    for position, parts in cuts:
        steps = jax.random.uniform(jax.random.fold_in(jax.random.fold_in(stream_key, 6), position), (parts,), jnp.float32, low / len(cuts), high / len(cuts))
        loudness = loudness * jnp.repeat(jnp.exp(steps), extent[position] // parts).reshape((-1,) + (1,) * (len(extent) - 1 - position))
    return loudness


def scatter_about(stream_key, extent, scale, reach, pieces=(), kind=jnp.bfloat16):
    values = jax.random.normal(stream_key, extent, jnp.float32) * scale
    if len(pieces) > 0:
        values = block_scale(stream_key, extent, pieces, -0.22, 0.18) * values
    return jnp.clip(values, min=-reach, max=reach).astype(kind)


def setup_inputs(seed: int = 0) -> dict:
    seeds = jax.random.split(jax.random.key(seed), 17)
    return {
        "x_in": scatter_about(seeds[0], (REQUESTS, LENGTH, EW), 1.0, 6.0, ((0, 8), (1, 16))),
        "dt_raw": scatter_about(seeds[1], (REQUESTS, LENGTH, HEADS_M), 1.0, 4.0, ((0, 8), (1, 16))),
        "bc_in": scatter_about(seeds[2], (REQUESTS, LENGTH, 2 * NS), 0.2, 1.1953125, ((0, 8), (1, 16))),
        "decay_rate": jnp.clip(jnp.exp(jax.random.uniform(seeds[3], (HEADS_M,), jnp.float32, math.log(2.441406286379788e-05), math.log(0.1))), 2.441406286379788e-05, 0.1),
        "skip_gain": jnp.clip(jax.random.uniform(seeds[4], (HEADS_M,), jnp.float32, 0.5, 1.5), 0.5, 1.5),
        "kv_pre": draw_kv_pre(jax.random.fold_in(seeds[16], 71), 0),
        "lengths": draw_lengths(jax.random.fold_in(seeds[16], 71), 0),
        "group_of": jax.random.permutation(seeds[7], REQUESTS).astype(jnp.int32),
        "slot_of": jax.vmap(lambda own: jax.random.permutation(own, PAGES))(jax.random.split(seeds[8], REQUESTS)).reshape((REQUESTS, PAGES)).astype(jnp.int32),
        "dec_x": scatter_about(seeds[9], (REQUESTS, STEPS, EW), 1.0, 6.0, ((0, 16), (2, 8))),
        "dec_dt": scatter_about(seeds[10], (REQUESTS, STEPS, HEADS_M), 1.0, 4.0, ((0, 16), (2, 8))),
        "dec_bc": scatter_about(seeds[11], (REQUESTS, STEPS, 2 * NS), 0.2, 1.1953125, ((0, 16),)),
        "dec_z": scatter_about(seeds[12], (REQUESTS, STEPS, EW), 1.0, 6.0, ((0, 16), (2, 8))),
        "norm_gain": jnp.clip(1.0 + 0.1 * jax.random.normal(seeds[13], (EW,), jnp.float32), 0.5, 1.5).astype(jnp.bfloat16),
        "dec_q": draw_dec_q(jax.random.fold_in(seeds[16], 71), 0),
        "dec_kv": scatter_about(seeds[15], (REQUESTS, STEPS, KVH * 2 * HD), 1.0, 6.0, ((0, 16), (2, 8))),
    }


highest = lax.Precision.HIGHEST

def round_half(values):
    return lax.optimization_barrier(values.astype(jnp.bfloat16)).astype(jnp.float32)

def block_apply(x_block, step_block, log_block, bc_block, live_block, carry_state, skip_gain):
    cumulative = jnp.cumsum(log_block, axis=0)
    b_rows = bc_block[:, :NS]
    c_rows = bc_block[:, NS:]
    scores = jnp.dot(c_rows, b_rows.T, preferred_element_type=jnp.float32)
    order = jnp.arange(BLK)
    causal = (order[:, None] >= order[None, :])[None]
    by_head = cumulative.T
    spread = jnp.where(causal, by_head[:, :, None] - by_head[:, None, :], 0.0)
    weights = jnp.where(causal, scores[None] * jnp.exp(spread) * step_block.T[:, None, :], 0.0)
    x_heads = x_block.reshape(BLK, HEADS_M, HP).astype(jnp.float32)
    within = jnp.einsum('hts,shp->thp', round_half(weights), x_heads)
    carried = jnp.exp(cumulative)[:, :, None] * jnp.einsum('tn,nhp->thp', c_rows.astype(jnp.float32), carry_state, precision=highest)
    output = ((within + carried + skip_gain[None, :, None] * x_heads) * live_block[:, None, None]).astype(jnp.bfloat16)
    to_end = jnp.exp(cumulative[-1][None, :] - cumulative) * step_block
    scaled = round_half(to_end[:, :, None] * x_heads)
    local_state = jnp.einsum('sn,shp->nhp', b_rows.astype(jnp.float32), scaled)
    updated = jnp.exp(cumulative[-1])[None, :, None] * carry_state + local_state
    return (output.reshape(BLK, EW), updated)

def reference(x_in, dt_raw, bc_in, decay_rate, skip_gain, kv_pre, lengths, group_of, slot_of, dec_x, dec_dt, dec_bc, dec_z, norm_gain, dec_q, dec_kv):
    count = LENGTH // BLK

    def prefill_request(inputs):
        x_rows, step_raw, bc_rows, length = inputs
        live = (jnp.arange(LENGTH) < length).astype(jnp.float32)
        step_size = jax.nn.softplus(step_raw.astype(jnp.float32)) * live[:, None]
        log_decay = -step_size * decay_rate[None, :]

        def advance(carry_state, block):
            x_block, step_block, log_block, bc_block, live_block = block
            output, updated = block_apply(x_block, step_block, log_block, bc_block, live_block, carry_state, skip_gain)
            return (updated, output)
        initial = jnp.zeros((NS, HEADS_M, HP), jnp.float32)
        final_state, outputs = lax.scan(advance, initial, (x_rows.reshape(count, BLK, EW), step_size.reshape(count, BLK, HEADS_M), log_decay.reshape(count, BLK, HEADS_M), bc_rows.reshape(count, BLK, 2 * NS), live.reshape(count, BLK)))
        return (outputs.reshape(LENGTH, EW), final_state)
    y_pre, finals = lax.map(prefill_request, (x_in, dt_raw, bc_in, lengths))
    r_of_group = jnp.zeros((REQUESTS,), jnp.int32).at[group_of].set(jnp.arange(REQUESTS, dtype=jnp.int32))
    scale = HD ** (-0.5)

    def decode_group(inputs):
        group, xs_rows, steps_raw, bc_rows, gates, queries, fresh = inputs
        request = r_of_group[group]
        length = lengths[request]
        carry_state = finals[request]
        mamba_rows = []
        for turn_index in range(STEPS):
            x_now = xs_rows[turn_index].astype(jnp.float32).reshape(HEADS_M, HP)
            step_now = jax.nn.softplus(steps_raw[turn_index].astype(jnp.float32))
            b_now = bc_rows[turn_index, :NS].astype(jnp.float32)
            c_now = bc_rows[turn_index, NS:].astype(jnp.float32)
            carry_state = jnp.exp(-step_now * decay_rate)[None, :, None] * carry_state + b_now[:, None, None] * (step_now[:, None] * x_now)[None]
            read_out = jnp.einsum('n,nhp->hp', c_now, carry_state, precision=highest) + skip_gain[:, None] * x_now
            gated = read_out * jax.nn.silu(gates[turn_index].astype(jnp.float32)).reshape(HEADS_M, HP)
            factor = lax.rsqrt(jnp.sum(gated * gated) / EW + 1e-05)
            mamba_rows.append(((gated * factor).reshape(EW) * norm_gain.astype(jnp.float32)).astype(jnp.bfloat16))
        valid = jnp.arange(LENGTH) < length
        cache = kv_pre[request].reshape(LENGTH, KVH, 2, HD).astype(jnp.float32)
        fresh_rows = fresh.reshape(STEPS, KVH, 2, HD).astype(jnp.float32)
        grouped = queries.reshape(STEPS, KVH, QH // KVH, HD).astype(jnp.float32)
        scores_old = jnp.einsum('skgd,lkd->skgl', grouped, cache[:, :, 0]) * scale
        scores_old = jnp.where(valid[None, None, None, :], scores_old, -1e+30)
        order = jnp.arange(STEPS)
        allowed = (order[None, :] <= order[:, None])[:, None, None, :]
        scores_new = jnp.where(allowed, jnp.einsum('skgd,jkd->skgj', grouped, fresh_rows[:, :, 0]) * scale, -1e+30)
        peak = jnp.maximum(lax.optimization_barrier(jnp.max(scores_old, axis=-1)), lax.optimization_barrier(jnp.max(scores_new, axis=-1)))[..., None]
        probs_old = jnp.exp(scores_old - peak)
        probs_new = jnp.exp(scores_new - peak)
        total = lax.optimization_barrier(jnp.sum(probs_old, axis=-1)) + lax.optimization_barrier(jnp.sum(probs_new, axis=-1))
        mixed = jnp.einsum('skgl,lkd->skgd', round_half(probs_old), cache[:, :, 1]) + jnp.einsum('skgj,jkd->skgd', round_half(probs_new), fresh_rows[:, :, 1])
        attended = (mixed / total[..., None]).astype(jnp.bfloat16).reshape(STEPS, QH * HD)
        kept = jnp.where(valid[:, None], kv_pre[request], jnp.zeros((), jnp.bfloat16)).reshape(PAGES, PAGE, KVH * 2 * HD)
        source = jnp.zeros((PAGES,), jnp.int32).at[slot_of[request]].set(jnp.arange(PAGES, dtype=jnp.int32))
        pool = kept[source].reshape(LENGTH, KVH * 2 * HD)
        return (jnp.stack(mamba_rows), carry_state.reshape(NS, EW), attended, pool)
    dec_mamba, dec_state, dec_attn, kv_pool = lax.map(decode_group, (jnp.arange(REQUESTS, dtype=jnp.int32), dec_x, dec_dt, dec_bc, dec_z, dec_q, dec_kv))
    return (y_pre, kv_pool, dec_mamba, dec_state, dec_attn)
```

```python
import jax
import jax.numpy as jnp
from jax import lax
from jax.experimental import pallas as pl
from jax.experimental.pallas import tpu as pltpu
from jax.sharding import PartitionSpec as P

HD = 128
BLK = 256
HP = 64
NS = 16
HEADS = 128
WIDTH = 8192
SEQ = 16
TP = 8
WC = 1024
LANE = 128
CHUNKS = WC // LANE
STEPS = WIDTH // WC
ROW = 4
PARTS = WIDTH // (ROW * LANE)
STATE_ROWS = 2 * PARTS * NS
FINAL_ROWS = PARTS * NS
DEC_X, DEC_Z, DEC_T = 2 * BLK, 2 * BLK + 16, 2 * BLK + 32
PAGE_ROWS = 2 * BLK + 48
F32 = jnp.float32
BF16 = jnp.bfloat16
MIB = 1024 * 1024
highest = lax.Precision.HIGHEST
ANY = pl.BlockSpec(memory_space=pl.ANY)
VM = pl.BlockSpec(memory_space=pltpu.VMEM)
SM = pl.BlockSpec(memory_space=pltpu.SMEM)


def params(mib=48):
    return pltpu.CompilerParams(vmem_limit_bytes=mib * MIB)


def cost(us):
    return pl.CostEstimate(flops=0, bytes_accessed=int(us * 3.0e6), transcendentals=0)


def softplus(v):
    return jnp.maximum(v, 0.0) + jnp.log1p(jnp.exp(-jnp.abs(v)))


def halves(v):
    high = v.astype(BF16)
    return high, (v - high.astype(F32)).astype(BF16)


def split_kernel(kv_ref, x_ref, z_ref, dt_ref, out_ref, token_ref):
    out_ref[0, :BLK, :] = kv_ref[0]
    out_ref[0, BLK : 2 * BLK, :] = kv_ref[1]

    def fold(rows):
        rows = rows.astype(F32)
        return jnp.concatenate([rows[:, q * 256 : (q + 1) * 256] for q in range(4)], axis=0)

    out_ref[0, DEC_X : DEC_X + 16, :] = fold(x_ref[0]).astype(BF16)
    out_ref[0, DEC_Z : DEC_Z + 16, :] = fold(z_ref[0]).astype(BF16)
    steps = dt_ref[0].astype(F32)
    steps = jnp.concatenate([steps, jnp.zeros((steps.shape[0], 256 - steps.shape[1]), F32)], axis=1)
    steps = jnp.concatenate([steps, jnp.zeros((12, 256), F32)], axis=0)
    out_ref[0, DEC_T : DEC_T + 16, :] = steps.astype(BF16)
    token_ref[0] = 0


def split_heads(kv_pre, dec_x, dec_z, dec_dt):
    whole = lambda h: (0, 0, 0)
    return pl.pallas_call(
        split_kernel,
        grid=(TP,),
        out_shape=[
            jax.ShapeDtypeStruct((TP, PAGE_ROWS, 2 * HD), BF16),
            jax.ShapeDtypeStruct((1,), jnp.int32),
        ],
        in_specs=[
            pl.BlockSpec((2, BLK, 2 * HD), lambda h: (0, 0, h)),
            pl.BlockSpec((1, 4, WC), whole),
            pl.BlockSpec((1, 4, WC), whole),
            pl.BlockSpec((1, 4, WC // HP), whole),
        ],
        out_specs=[pl.BlockSpec((1, PAGE_ROWS, 2 * HD), lambda h: (h, 0, 0)), SM],
        cost_estimate=cost(2),
        compiler_params=params(),
        name="split_heads",
    )(kv_pre, dec_x, dec_z, dec_dt)


def spread_matrix(ebig):
    rows = lax.broadcasted_iota(jnp.int32, ebig.shape, 0)
    cols = lax.broadcasted_iota(jnp.int32, ebig.shape, 1)
    ebig[...] = jnp.where((rows & (HEADS - 1)) == (cols >> 6), 1.0, 0.0).astype(BF16)


def spread_rows(ebig, j):
    start = pl.multiple_of(HEADS - (WC // HP) * j, 16)
    return ebig[pl.ds(start, 2 * HEADS), :]


def decays(len_ref, dt_ref, rate_ref, p):
    prompt = lax.axis_index("tp") * 2 + p
    live = jnp.where(len_ref[prompt] > lax.axis_index("seq") * BLK, 1.0, 0.0).astype(F32)
    step = softplus(dt_ref[p].astype(F32)) * live
    rows = lax.broadcasted_iota(jnp.int32, (BLK, BLK), 0)
    cols = lax.broadcasted_iota(jnp.int32, (BLK, BLK), 1)
    tri = jnp.where(rows >= cols, 1.0, 0.0).astype(F32)
    cum = jnp.dot(tri, -step * rate_ref[...], precision=highest, preferred_element_type=F32)
    mid = 0.5 * cum[BLK - 1 :, :]
    return live, step, cum - mid, mid


def block_copies(hbm, buf, sem, out=False):
    copies = []
    for p in range(2):
        for j in range(STEPS):
            cols = pl.ds(j * WC, WC)
            ends = (hbm.at[p, :, cols], buf.at[p, :, cols])
            copies.append(pltpu.make_async_copy(*(ends[::-1] if out else ends), sem.at[p * STEPS + j]))
    return copies


def block_copy(hbm, buf, sem, p, j, out=False):
    cols = pl.ds(pl.multiple_of(j * WC, WC), WC)
    ends = (hbm.at[p, :, cols], buf.at[p, :, cols])
    return pltpu.make_async_copy(*(ends[::-1] if out else ends), sem.at[p * STEPS + j])


def local_kernel(len_ref, x_hbm, dt_ref, bc_ref, rate_ref, *refs):
    outs, (stage, ft, bt, x_buf, sem) = refs[:ROW], refs[ROW:]
    for c in block_copies(x_hbm, x_buf, sem):
        c.start()
    lane = lax.broadcasted_iota(jnp.int32, (NS, LANE), 1)
    row = lax.broadcasted_iota(jnp.int32, (NS, HEADS), 0)
    heads = WC // HP
    dec = jnp.zeros((NS, HEADS), F32)
    for p in range(2):
        live, step, rel, mid = decays(len_ref, dt_ref, rate_ref, p)
        ft[p] = jnp.transpose(jnp.exp(-rel) * step)
        bt[p] = jnp.transpose(bc_ref[p].astype(F32))[:NS]
        high, low = halves(jnp.exp(mid))
        dec = jnp.where(row == p, high.astype(F32), jnp.where(row == 2 + p, low.astype(F32), dec))
    for s in range(ROW):
        stage[s, STATE_ROWS:, :] = dec.astype(BF16)
    for p in range(2):

        def body(j, carry):
            quarter, part = lax.div(j, 2), lax.rem(j, 2)
            block_copy(x_hbm, x_buf, sem, p, j).wait()
            fj = ft[p, pl.ds(pl.multiple_of(j * heads, heads), heads), :]
            for u in range(WC // 256):
                left = jnp.concatenate([bt[p] * fj[u * 4 + h : u * 4 + h + 1, :] for h in range(4)], axis=0)
                cols = pl.ds(pl.multiple_of(j * WC + u * 256, 256), 256)
                prod = jnp.dot(left.astype(BF16), x_buf[p, :, cols], preferred_element_type=F32)
                for v in range(2):
                    cols = slice(v * LANE, (v + 1) * LANE)
                    first = prod[2 * v * NS : (2 * v + 1) * NS, cols]
                    second = prod[(2 * v + 1) * NS : (2 * v + 2) * NS, cols]
                    local = jnp.where(lane < HP, first, second).astype(BF16)
                    at = ((p * 2 + part) * CHUNKS + u * 2 + v) * NS
                    stage[quarter, pl.ds(pl.multiple_of(at, NS), NS), :] = local
            return carry

        lax.fori_loop(0, STEPS, body, 0)
    y = lax.rem(lax.axis_index("seq"), ROW)
    for o in range(ROW):
        outs[o][...] = stage[lax.rem(y + o, ROW)]


def local_states(lengths, x_in, dt_raw, bc_in, rate):
    return pl.pallas_call(
        local_kernel,
        out_shape=[jax.ShapeDtypeStruct((STATE_ROWS + NS, LANE), BF16)] * ROW,
        in_specs=[SM, ANY, VM, VM, VM],
        out_specs=[VM] * ROW,
        scratch_shapes=[
            pltpu.VMEM((ROW, STATE_ROWS + NS, LANE), BF16),
            pltpu.VMEM((2, HEADS, BLK), F32),
            pltpu.VMEM((2, NS, BLK), F32),
            pltpu.VMEM((2, BLK, WIDTH), BF16),
            pltpu.SemaphoreType.DMA((2 * STEPS,)),
        ],
        cost_estimate=cost(6),
        compiler_params=params(),
        name="local_states",
    )(lengths, x_in, dt_raw, bc_in, rate)


def place(arrays, scratch, me):
    for o in range(ROW):
        scratch[lax.rem(me + ROW - o, ROW)] = arrays[o][...]


def spread_decays(blocks, y):
    rows = lax.broadcasted_iota(jnp.int32, (HEADS, PARTS * LANE), 0)
    cols = lax.broadcasted_iota(jnp.int32, (HEADS, PARTS * LANE), 1)
    pick = jnp.where(rows == y * (PARTS * 2) + (cols >> 6), 1.0, 0.0).astype(BF16)
    return jnp.dot(jnp.concatenate(blocks, axis=0), pick, preferred_element_type=F32)


def decay_of(wide, block, p, c):
    cols = slice(c * LANE, (c + 1) * LANE)
    return wide[block * NS + p : block * NS + p + 1, cols] + wide[block * NS + 2 + p : block * NS + 3 + p, cols]


def groups():
    return [(p, c, (p * PARTS + c) * NS) for p in range(2) for c in range(PARTS)]


def row_kernel(*refs):
    ins, out, scr = refs[:ROW], refs[ROW], refs[ROW + 1]
    y = lax.rem(lax.axis_index("seq"), ROW)
    place(ins, scr, y)
    wide = spread_decays([scr[b, STATE_ROWS:, :] for b in range(ROW)], y)
    for p, c, at in groups():
        state = jnp.zeros((NS, LANE), F32)
        for b in range(ROW):
            half = decay_of(wide, b, p, c)
            state = half * (half * state + scr[b, at : at + NS, :].astype(F32))
        out[at : at + NS, :] = state.astype(BF16)
    compact = [scr[b, STATE_ROWS:, :].astype(F32) for b in range(ROW)]
    row = lax.broadcasted_iota(jnp.int32, (NS, LANE), 0)
    dec = jnp.zeros((NS, LANE), F32)
    for p in range(2):
        all_rows = jnp.ones((1, LANE), F32)
        for b in range(ROW):
            half = compact[b][p : p + 1, :] + compact[b][2 + p : 3 + p, :]
            all_rows = all_rows * (half * half)
        high, low = halves(all_rows)
        dec = jnp.where(row == p, high.astype(F32), jnp.where(row == 2 + p, low.astype(F32), dec))
    out[STATE_ROWS:, :] = dec.astype(BF16)


def row_totals(blocks):
    return pl.pallas_call(
        row_kernel,
        out_shape=jax.ShapeDtypeStruct((STATE_ROWS + NS, LANE), BF16),
        in_specs=[VM] * ROW,
        out_specs=VM,
        scratch_shapes=[pltpu.VMEM((ROW, STATE_ROWS + NS, LANE), BF16)],
        cost_estimate=cost(1),
        compiler_params=params(),
        name="row_totals",
    )(*blocks)


def enter_kernel(group_ref, *refs):
    blocks, totals, outs = refs[:ROW], refs[ROW : 2 * ROW], refs[2 * ROW : 3 * ROW]
    scr, rows, start, stage = refs[3 * ROW :]
    me = lax.axis_index("seq")
    x, y = lax.div(me, ROW), lax.rem(me, ROW)
    place(blocks, scr, y)
    place(totals, rows, x)
    wide = spread_decays(
        [scr[b, STATE_ROWS:, :] for b in range(ROW)] + [rows[b, STATE_ROWS:, :] for b in range(ROW)], y
    )
    for p, c, at in groups():
        state = jnp.zeros((NS, LANE), F32)
        for b in range(ROW):
            start[b, at : at + NS, :] = state
            state = decay_of(wide, ROW + b, p, c) * state + rows[b, at : at + NS, :].astype(F32)
        start[ROW, at : at + NS, :] = state
    for p, c, at in groups():
        state = start[x, at : at + NS, :]
        for b in range(ROW):
            half = decay_of(wide, b, p, c)
            entering = half * state
            stage[b, at : at + NS, :] = entering.astype(BF16)
            state = half * (entering + scr[b, at : at + NS, :].astype(F32))
    second = group_ref[lax.axis_index("tp") * 2 + 1]
    for b in range(ROW):
        at = jnp.where(second == x * ROW + b, FINAL_ROWS, 0)
        final = start[ROW, pl.ds(pl.multiple_of(at, FINAL_ROWS), FINAL_ROWS), :]
        stage[b, STATE_ROWS:, :] = final.astype(BF16)
    for o in range(ROW):
        outs[o][...] = stage[lax.rem(y + o, ROW)]


def enter_states(group_of, blocks, totals):
    return pl.pallas_call(
        enter_kernel,
        out_shape=[jax.ShapeDtypeStruct((STATE_ROWS + FINAL_ROWS, LANE), BF16)] * ROW,
        in_specs=[SM] + [VM] * (2 * ROW),
        out_specs=[VM] * ROW,
        scratch_shapes=[
            pltpu.VMEM((ROW, STATE_ROWS + NS, LANE), BF16),
            pltpu.VMEM((ROW, STATE_ROWS + NS, LANE), BF16),
            pltpu.VMEM((ROW + 1, STATE_ROWS, LANE), F32),
            pltpu.VMEM((ROW, STATE_ROWS + FINAL_ROWS, LANE), BF16),
        ],
        cost_estimate=cost(2),
        compiler_params=params(),
        name="enter_states",
    )(group_of, *blocks, *totals)


def order_kernel(group_ref, pages, out):
    for r in range(SEQ):
        at = r % 2 * BLK
        out[group_ref[r]] = pages[r // 2, at : at + BLK, :]


def order_pages(group_of, pages):
    return pl.pallas_call(
        order_kernel,
        out_shape=jax.ShapeDtypeStruct((SEQ, BLK, 2 * HD), BF16),
        in_specs=[SM, VM],
        out_specs=VM,
        cost_estimate=cost(2),
        compiler_params=params(),
        name="order_pages",
    )(group_of, pages)


def output_kernel(len_ref, x_hbm, dt_ref, bc_ref, rate_ref, skip_ref, *refs):
    enters, y_hbm, (ebig, both, mix, enter, x_buf, y_buf, sem, out_sem) = refs[:ROW], refs[ROW], refs[ROW + 1 :]
    for c in block_copies(x_hbm, x_buf, sem):
        c.start()
    spread_matrix(ebig)
    y = lax.rem(lax.axis_index("seq"), ROW)
    for o in range(ROW):
        enter[lax.rem(y + ROW - o, ROW)] = enters[o][:STATE_ROWS, :]
    rows = lax.broadcasted_iota(jnp.int32, (BLK, BLK), 0)
    cols = lax.broadcasted_iota(jnp.int32, (BLK, BLK), 1)
    for p in range(2):
        live, step, rel, mid = decays(len_ref, dt_ref, rate_ref, p)
        factors = [jnp.exp(-rel) * step, jnp.exp(rel) * live, jnp.broadcast_to(skip_ref[...] * live, (NS, HEADS))]
        for at, v in zip((0, BLK, 2 * BLK), factors):
            high, low = halves(v)
            both[p, at : at + v.shape[0], :HEADS] = high
            both[p, at : at + v.shape[0], HEADS:] = low
        scores = lax.dot_general(
            bc_ref[p, :, NS:], bc_ref[p, :, :NS], (((1,), (1,)), ((), ())), preferred_element_type=F32
        )
        mix[p] = jnp.where(rows >= cols, scores, 0.0).astype(BF16)
    for p in range(2):

        def body(j, carry):
            block_copy(x_hbm, x_buf, sem, p, j).wait()
            at = pl.ds(pl.multiple_of(j * WC, WC), WC)
            ej = spread_rows(ebig, j)
            x = x_buf[p, :, at].astype(F32)
            factor = jnp.dot(both[p], ej, preferred_element_type=F32)
            xp = (x * factor[:BLK]).astype(BF16)
            first = (p * 2 + lax.rem(j, 2)) * CHUNKS * NS
            entering = enter[lax.div(j, 2), pl.ds(pl.multiple_of(first, CHUNKS * NS), CHUNKS * NS), :]
            entering = jnp.concatenate([entering[i * NS : (i + 1) * NS] for i in range(CHUNKS)], axis=1)
            total = jnp.dot(mix[p], xp, preferred_element_type=F32) + jnp.dot(
                bc_ref[p, :, NS:], entering, preferred_element_type=F32
            )
            y_buf[p, :, at] = (factor[BLK : 2 * BLK] * total + factor[2 * BLK : 2 * BLK + 1] * x).astype(BF16)
            block_copy(y_hbm, y_buf, out_sem, p, j, out=True).start()
            return carry

        lax.fori_loop(0, STEPS, body, 0)
    for c in block_copies(y_hbm, y_buf, out_sem, out=True):
        c.wait()


def block_outputs(lengths, x_in, dt_raw, bc_in, rate, skip, entering):
    return pl.pallas_call(
        output_kernel,
        out_shape=jax.ShapeDtypeStruct((2, BLK, WIDTH), BF16),
        in_specs=[SM, ANY] + [VM] * (4 + ROW),
        out_specs=ANY,
        scratch_shapes=[
            pltpu.VMEM((3 * HEADS, WC), BF16),
            pltpu.VMEM((2, 2 * BLK + NS, 2 * HEADS), BF16),
            pltpu.VMEM((2, BLK, BLK), BF16),
            pltpu.VMEM((ROW, STATE_ROWS, LANE), BF16),
            pltpu.VMEM((2, BLK, WIDTH), BF16),
            pltpu.VMEM((2, BLK, WIDTH), BF16),
            pltpu.SemaphoreType.DMA((2 * STEPS,)),
            pltpu.SemaphoreType.DMA((2 * STEPS,)),
        ],
        cost_estimate=cost(12),
        compiler_params=params(),
        name="block_outputs",
    )(lengths, x_in, dt_raw, bc_in, rate, skip, *entering)


def my_prompt(group_ref):
    mine = lax.axis_index("seq")
    prompt = jnp.int32(0)
    for r in range(SEQ):
        prompt = jnp.where(group_ref[r] == mine, r, prompt)
    return prompt


def attend_kernel(
    group_ref, len_ref, slot_ref, recv, q_ref, fresh, pool, out_ref, zeros, sem
):
    prompt = my_prompt(group_ref)
    length = len_ref[prompt]
    zeros[...] = jnp.zeros(zeros.shape, BF16)

    def page_copy(s, live):
        at = pl.ds(pl.multiple_of(slot_ref[prompt, s] * BLK, BLK), BLK)
        source = recv.at[s] if live else zeros
        return pltpu.make_async_copy(source, pool.at[0, at, :], sem.at[s])

    for s in range(SEQ):

        @pl.when(length > s * BLK)
        def _():
            page_copy(s, True).start()

        @pl.when(length <= s * BLK)
        def _():
            page_copy(s, False).start()

    q = q_ref[...]
    scale = HD**-0.5
    contract = (((1,), (1,)), ((), ()))
    rows = lax.broadcasted_iota(jnp.int32, (q.shape[0], fresh.shape[0]), 0)
    cols = lax.broadcasted_iota(jnp.int32, (q.shape[0], fresh.shape[0]), 1)
    new = lax.dot_general(q, fresh[:, :HD], contract, preferred_element_type=F32) * scale
    new = jnp.where(cols <= (rows & 3), new, -1e30)
    peak = jnp.max(new, axis=1, keepdims=True)
    old = []
    for s in range(SEQ):
        part = lax.dot_general(q, recv[s, :, :HD], contract, preferred_element_type=F32) * scale
        part = jnp.where(length > s * BLK, part, -1e30)
        old.append(part)
        peak = jnp.maximum(peak, jnp.max(part, axis=1, keepdims=True))
    prob = jnp.exp(new - peak)
    total = jnp.sum(prob, axis=1, keepdims=True)
    mixed = jnp.dot(prob.astype(BF16), fresh[:, HD:], preferred_element_type=F32)
    for s in range(SEQ):
        prob = jnp.exp(old[s] - peak)
        total = total + jnp.sum(prob, axis=1, keepdims=True)
        mixed = mixed + jnp.dot(prob.astype(BF16), recv[s, :, HD:], preferred_element_type=F32)
    result = mixed / total
    steps = out_ref.shape[1]
    for h in range(q.shape[0] // steps):
        out_ref[0, :, h * HD : (h + 1) * HD] = result[h * steps : (h + 1) * steps].astype(BF16)
    for s in range(SEQ):
        page_copy(s, True).wait()


def attend(group_of, lengths, slot_of, recv, queries, fresh):
    return pl.pallas_call(
        attend_kernel,
        out_shape=[
            jax.ShapeDtypeStruct((1, SEQ * BLK, 2 * HD), BF16),
            jax.ShapeDtypeStruct((1, 4, WC), BF16),
        ],
        in_specs=[SM, SM, SM, VM, VM, VM],
        out_specs=[ANY, VM],
        scratch_shapes=[pltpu.VMEM((BLK, 2 * HD), BF16), pltpu.SemaphoreType.DMA((SEQ,))],
        cost_estimate=cost(5),
        compiler_params=params(),
        name="attend",
    )(group_of, lengths, slot_of, recv, queries, fresh)


def decode_kernel(inputs, bct_ref, rate_ref, skip_ref, *refs):
    finals, outs, (fin, res) = refs[:ROW], refs[ROW : ROW + TP], refs[ROW + TP :]
    me = lax.axis_index("tp")
    y = lax.rem(lax.axis_index("seq"), ROW)
    for o in range(ROW):
        fin[lax.rem(y + ROW - o, ROW)] = finals[o][STATE_ROWS:, :]
    heads = WC // HP
    rows = lax.broadcasted_iota(jnp.int32, (heads, WC), 0)
    cols = lax.broadcasted_iota(jnp.int32, (heads, WC), 1)
    spread = jnp.where(rows == (cols >> 6), 1.0, 0.0).astype(F32)
    raw = [inputs[t, DEC_T : DEC_T + 16, :].astype(F32)[:4, :heads] for t in range(TP)]
    step = softplus(jnp.concatenate(raw, axis=0))
    rates = jnp.concatenate([jnp.broadcast_to(rate_ref[t : t + 1], (4, heads)) for t in range(TP)], axis=0)
    small = jnp.concatenate([step, jnp.exp(-step * rates), skip_ref[...]], axis=0)
    wide = jnp.dot(small, spread, precision=highest, preferred_element_type=F32)

    def unfold(rows):
        return jnp.concatenate([rows[q * 4 : (q + 1) * 4] for q in range(4)], axis=1)

    sums = [jnp.zeros((1, 1), F32)] * 4
    for t in range(TP):
        x = unfold(inputs[t, DEC_X : DEC_X + 16, :].astype(F32))
        z = unfold(inputs[t, DEC_Z : DEC_Z + 16, :].astype(F32))
        gate = z / (1.0 + jnp.exp(-z))
        chunks = [t * CHUNKS + i for i in range(CHUNKS)]
        state = jnp.concatenate(
            [fin[k // PARTS, k % PARTS * NS : (k % PARTS + 1) * NS, :].astype(F32) for k in chunks], axis=1
        )
        skip = wide[8 * TP + t : 8 * TP + t + 1]
        for k in range(4):
            b_col = bct_ref[:NS, k : k + 1]
            c_col = bct_ref[NS:, k : k + 1]
            wide_step = wide[4 * t + k : 4 * t + k + 1]
            fade = wide[4 * TP + 4 * t + k : 4 * TP + 4 * t + k + 1]
            state = fade * state + b_col * (wide_step * x[k : k + 1])
            read = jnp.sum(c_col * state, axis=0, keepdims=True) + skip * x[k : k + 1]
            v = read * gate[k : k + 1]
            res[t, NS + k : NS + k + 1, :] = v
            sums[k] = sums[k] + jnp.sum(v * v, axis=1, keepdims=True)
        res[t, :NS, :] = state
    factor = jnp.concatenate([lax.rsqrt(sums[k] / WIDTH + 1e-05) for k in range(4)], axis=0)
    for t in range(TP):
        res[t, NS : NS + 4, :] = res[t, NS : NS + 4, :] * factor
        res[t, NS + 4 :, :] = jnp.zeros((4, WC), F32)
    for o in range(TP):
        outs[o][...] = res[lax.rem(me + o, TP)]


def decode(inputs, bct, rate, skip, finals):
    return pl.pallas_call(
        decode_kernel,
        out_shape=[jax.ShapeDtypeStruct((NS + 8, WC), F32)] * TP,
        in_specs=[VM] * (4 + ROW),
        out_specs=[VM] * TP,
        scratch_shapes=[
            pltpu.VMEM((ROW, FINAL_ROWS, LANE), BF16),
            pltpu.VMEM((TP, NS + 8, WC), F32),
        ],
        cost_estimate=cost(4),
        compiler_params=params(),
        name="decode",
    )(inputs, bct, rate, skip, *finals)


def pick_kernel(group_ref, gain_ref, *refs):
    results, (state_ref, out_ref) = refs[:TP], refs[TP:]
    holder = lax.div(my_prompt(group_ref), 2)
    distance = lax.rem(lax.axis_index("tp") + TP - holder, TP)
    for o in range(TP):

        @pl.when(distance == o)
        def _():
            state_ref[0] = results[o][:NS, :]
            out_ref[0] = (results[o][NS : NS + 4, :] * gain_ref[...].astype(F32)).astype(BF16)


def pick(group_of, gain, results):
    return pl.pallas_call(
        pick_kernel,
        out_shape=[
            jax.ShapeDtypeStruct((1, NS, WC), F32),
            jax.ShapeDtypeStruct((1, 4, WC), BF16),
        ],
        in_specs=[SM] + [VM] * (1 + TP),
        out_specs=[VM] * 2,
        cost_estimate=cost(1),
        compiler_params=params(),
        name="pick",
    )(group_of, gain, *results)


def rotate(arrays):
    return [arrays[0]] + [
        lax.ppermute(arrays[o], "tp", [(i, (i + o) % TP) for i in range(TP)]) for o in range(1, TP)
    ]


def along_y(arrays):
    moves = [[(x * ROW + y, x * ROW + (y + o) % ROW) for x in range(ROW) for y in range(ROW)] for o in range(ROW)]
    return [arrays[0]] + [lax.ppermute(arrays[o], "seq", moves[o]) for o in range(1, ROW)]


def along_x(arrays):
    moves = [[(i, (i + o * ROW) % SEQ) for i in range(SEQ)] for o in range(ROW)]
    return [arrays[0]] + [lax.ppermute(arrays[o], "seq", moves[o]) for o in range(1, ROW)]


def shards(
    x_in, dt_raw, bc_in, decay_rate, skip_gain, kv_pre, lengths, group_of, slot_of,
    dec_x, dec_dt, dec_bc, dec_z, norm_gain, dec_q, dec_kv,
):
    rate = decay_rate.reshape(1, HEADS)
    skip = skip_gain.reshape(1, HEADS)
    bct = jnp.transpose(dec_bc[0].astype(F32))
    queries = jnp.transpose(dec_q.reshape(4, -1, HD), (1, 0, 2)).reshape(-1, HD)
    fresh = jnp.concatenate([dec_kv[0], jnp.zeros((12, 2 * HD), BF16)], axis=0)
    gain = norm_gain.reshape(1, -1)

    sent, token = split_heads(kv_pre, dec_x, dec_z, dec_dt)
    pages = lax.all_to_all(sent, "tp", split_axis=0, concat_axis=0, tiled=True)
    early_lengths, token = lax.optimization_barrier((lengths, token))
    blocks = along_y(local_states(early_lengths, x_in, dt_raw, bc_in, rate))
    totals = along_x([row_totals(blocks)] * ROW)
    pages, totals = lax.optimization_barrier((pages, totals))
    entering = along_y(enter_states(group_of, blocks, totals))
    recv = lax.all_to_all(order_pages(group_of, pages), "seq", split_axis=0, concat_axis=0, tiled=True)
    results = decode(pages, bct, decay_rate.reshape(TP, -1), skip_gain.reshape(TP, -1), entering)
    dec_state, dec_mamba = pick(group_of, gain, rotate(results))
    y_pre = block_outputs(lengths, x_in, dt_raw, bc_in, rate, skip, entering)
    kv_pool, dec_attn = attend(group_of, lengths, slot_of, recv, queries, fresh)
    return (y_pre, kv_pool, dec_mamba, dec_state, dec_attn)


def solution(mesh):
    return jax.shard_map(
        shards,
        mesh=mesh,
        in_specs=(
            P("tp", "seq", None),
            P("tp", "seq", None),
            P("tp", "seq", None),
            P(),
            P(),
            P("tp", "seq", None),
            P(),
            P(),
            P(),
            P("seq", None, "tp"),
            P("seq", None, "tp"),
            P("seq", None, None),
            P("seq", None, "tp"),
            P("tp"),
            P("seq", None, "tp"),
            P("seq", None, "tp"),
        ),
        out_specs=(
            P("tp", "seq", None),
            P("seq", None, "tp"),
            P("seq", None, "tp"),
            P("seq", None, "tp"),
            P("seq", None, "tp"),
        ),
        check_vma=False,
    )
```

```python
import jax
import jax.numpy as jnp
from jax import lax
from jax.experimental import pallas as pl
from jax.experimental.pallas import tpu as pltpu
from jax.sharding import PartitionSpec as P

HD = 128
BLK = 256
HP = 64
NS = 16
HEADS = 128
WIDTH = 8192
SEQ = 16
TP = 8
WC = 1024
LANE = 128
CHUNKS = WC // LANE
STEPS = WIDTH // WC
ROW = 4
PARTS = WIDTH // (ROW * LANE)
STATE_ROWS = 2 * PARTS * NS
FINAL_ROWS = PARTS * NS
DEC_X = 2 * BLK
PAGE_ROWS = 2 * BLK + 48
F32 = jnp.float32
BF16 = jnp.bfloat16
MIB = 1024 * 1024
highest = lax.Precision.HIGHEST
ANY = pl.BlockSpec(memory_space=pl.ANY)
VM = pl.BlockSpec(memory_space=pltpu.VMEM)
SM = pl.BlockSpec(memory_space=pltpu.SMEM)


def params(mib=44):
    return pltpu.CompilerParams(vmem_limit_bytes=mib * MIB)


def cost(us):
    return pl.CostEstimate(flops=0, bytes_accessed=int(us * 3.0e6), transcendentals=0)


def softplus(v):
    return jnp.maximum(v, 0.0) + jnp.log1p(jnp.exp(-jnp.abs(v)))


def halves(v):
    high = v.astype(BF16)
    return high, (v - high.astype(F32)).astype(BF16)


def fetch(pairs, sem, first=0):
    copies = [pltpu.make_async_copy(src, dst, sem.at[first + n]) for n, (src, dst) in enumerate(pairs)]
    for c in copies:
        c.start()
    return copies


def split_start(kv, x_hbm, z_hbm, dt_hbm, out, buf, x_buf, z_buf, dt_buf, rows, sem, out_sem):
    small = fetch([(x_hbm.at[0], x_buf), (z_hbm.at[0], z_buf), (dt_hbm.at[0], dt_buf)], sem, 2 * TP)
    parts = [(i, pl.ds(q * BLK // 4, BLK // 4)) for i in range(2) for q in range(4)]
    arrive = fetch([(kv.at[part], buf.at[part]) for part in parts], sem)

    def fold(part):
        part = part.astype(F32)
        return jnp.concatenate([part[:, q * 256 : (q + 1) * 256] for q in range(4)], axis=0)

    def finish():
        for c in small:
            c.wait()
        rows[:16, :] = fold(x_buf[...]).astype(BF16)
        rows[16:32, :] = fold(z_buf[...]).astype(BF16)
        steps = dt_buf[...].astype(F32)
        steps = jnp.concatenate([steps, jnp.zeros((steps.shape[0], 256 - steps.shape[1]), F32)], axis=1)
        steps = jnp.concatenate([steps, jnp.zeros((12, 256), F32)], axis=0)
        rows[32:, :] = steps.astype(BF16)
        leave = fetch([(rows, out.at[h, pl.ds(DEC_X, 48), :]) for h in range(TP)], out_sem)
        for i in range(2):
            for c in arrive[4 * i : 4 * i + 4]:
                c.wait()
            heads = [(h, pl.ds(h * 2 * HD, 2 * HD)) for h in range(TP)]
            leave += fetch(
                [(buf.at[i, :, cols], out.at[h, pl.ds(i * BLK, BLK), :]) for h, cols in heads], out_sem, TP * (1 + i)
            )
        return leave

    return finish


def spread_matrix(ebig):
    rows = lax.broadcasted_iota(jnp.int32, ebig.shape, 0)
    cols = lax.broadcasted_iota(jnp.int32, ebig.shape, 1)
    ebig[...] = jnp.where((rows & (HEADS - 1)) == (cols >> 6), 1.0, 0.0).astype(BF16)


def spread_rows(ebig, j):
    start = pl.multiple_of(HEADS - (WC // HP) * j, 16)
    return ebig[pl.ds(start, 2 * HEADS), :]


def decays(len_ref, dt_ref, rate_ref, p):
    prompt = lax.axis_index("tp") * 2 + p
    live = jnp.where(len_ref[prompt] > lax.axis_index("seq") * BLK, 1.0, 0.0).astype(F32)
    step = softplus(dt_ref[p].astype(F32)) * live
    rows = lax.broadcasted_iota(jnp.int32, (BLK, BLK), 0)
    cols = lax.broadcasted_iota(jnp.int32, (BLK, BLK), 1)
    tri = jnp.where(rows >= cols, 1.0, 0.0).astype(F32)
    cum = jnp.dot(tri, -step * rate_ref[...], precision=highest, preferred_element_type=F32)
    mid = 0.5 * cum[BLK - 1 :, :]
    return live, step, cum - mid, mid


def block_copies(hbm, buf, sem, out=False):
    copies = []
    for p in range(2):
        for j in range(STEPS):
            cols = pl.ds(j * WC, WC)
            ends = (hbm.at[p, :, cols], buf.at[p, :, cols])
            copies.append(pltpu.make_async_copy(*(ends[::-1] if out else ends), sem.at[p * STEPS + j]))
    return copies


def block_copy(hbm, buf, sem, p, j, out=False):
    cols = pl.ds(pl.multiple_of(j * WC, WC), WC)
    ends = (hbm.at[p, :, cols], buf.at[p, :, cols])
    return pltpu.make_async_copy(*(ends[::-1] if out else ends), sem.at[p * STEPS + j])


def local_kernel(len_ref, x_hbm, dt_hbm, bc_hbm, rate_hbm, kv, dx_hbm, dz_hbm, ddt_hbm, *refs):
    outs, split, (stage, ft, bt, x_buf, dt_ref, bc_ref, rate_ref, sem), rest = (
        refs[:ROW],
        refs[ROW],
        refs[ROW + 1 : ROW + 9],
        refs[ROW + 9 :],
    )
    small = fetch([(dt_hbm, dt_ref), (bc_hbm, bc_ref), (rate_hbm, rate_ref)], sem, 2 * STEPS)
    finish = split_start(kv, dx_hbm, dz_hbm, ddt_hbm, split, *rest)
    for c in block_copies(x_hbm, x_buf, sem):
        c.start()
    for c in small:
        c.wait()
    lane = lax.broadcasted_iota(jnp.int32, (NS, LANE), 1)
    row = lax.broadcasted_iota(jnp.int32, (NS, HEADS), 0)
    heads = WC // HP
    dec = jnp.zeros((NS, HEADS), F32)
    for p in range(2):
        live, step, rel, mid = decays(len_ref, dt_ref, rate_ref, p)
        ft[p] = jnp.transpose(jnp.exp(-rel) * step)
        bt[p] = bc_ref[p, :NS, :].astype(F32)
        high, low = halves(jnp.exp(mid))
        dec = jnp.where(row == p, high.astype(F32), jnp.where(row == 2 + p, low.astype(F32), dec))
    for s in range(ROW):
        stage[s, STATE_ROWS:, :] = dec.astype(BF16)
    for p in range(2):
        if p == 1:
            leave = finish()

        def body(j, carry):
            quarter, part = lax.div(j, 2), lax.rem(j, 2)
            block_copy(x_hbm, x_buf, sem, p, j).wait()
            fj = ft[p, pl.ds(pl.multiple_of(j * heads, heads), heads), :]
            for u in range(WC // 256):
                left = jnp.concatenate([bt[p] * fj[u * 4 + h : u * 4 + h + 1, :] for h in range(4)], axis=0)
                cols = pl.ds(pl.multiple_of(j * WC + u * 256, 256), 256)
                prod = jnp.dot(left.astype(BF16), x_buf[p, :, cols], preferred_element_type=F32)
                for v in range(2):
                    cols = slice(v * LANE, (v + 1) * LANE)
                    first = prod[2 * v * NS : (2 * v + 1) * NS, cols]
                    second = prod[(2 * v + 1) * NS : (2 * v + 2) * NS, cols]
                    local = jnp.where(lane < HP, first, second).astype(BF16)
                    at = ((p * 2 + part) * CHUNKS + u * 2 + v) * NS
                    stage[quarter, pl.ds(pl.multiple_of(at, NS), NS), :] = local
            return carry

        lax.fori_loop(0, STEPS, body, 0)
    y = lax.rem(lax.axis_index("seq"), ROW)
    for o in range(ROW):
        outs[o][...] = stage[lax.rem(y + o, ROW)]
    for c in leave:
        c.wait()


def local_states(lengths, x_in, dt_raw, bc_in, rate, kv_pre, dec_x, dec_z, dec_dt):
    return pl.pallas_call(
        local_kernel,
        out_shape=[jax.ShapeDtypeStruct((STATE_ROWS + NS, LANE), BF16)] * ROW
        + [jax.ShapeDtypeStruct((TP, PAGE_ROWS, 2 * HD), BF16)],
        in_specs=[SM] + [ANY] * 8,
        out_specs=[VM] * ROW + [ANY],
        scratch_shapes=[
            pltpu.VMEM((ROW, STATE_ROWS + NS, LANE), BF16),
            pltpu.VMEM((2, HEADS, BLK), F32),
            pltpu.VMEM((2, NS, BLK), F32),
            pltpu.VMEM((2, BLK, WIDTH), BF16),
            pltpu.VMEM((2, BLK, HEADS), BF16),
            pltpu.VMEM((2, 2 * NS, BLK), BF16),
            pltpu.VMEM((1, HEADS), F32),
            pltpu.SemaphoreType.DMA((2 * STEPS + 3,)),
            pltpu.VMEM((2, BLK, TP * 2 * HD), BF16),
            pltpu.VMEM((4, WC), BF16),
            pltpu.VMEM((4, WC), BF16),
            pltpu.VMEM((4, WC // HP), BF16),
            pltpu.VMEM((48, 2 * HD), BF16),
            pltpu.SemaphoreType.DMA((2 * TP + 3,)),
            pltpu.SemaphoreType.DMA((3 * TP,)),
        ],
        cost_estimate=cost(6),
        compiler_params=params(60),
        name="local_states",
    )(lengths, x_in, dt_raw, bc_in, rate, kv_pre, dec_x, dec_z, dec_dt)


def place(arrays, scratch, me):
    for o in range(ROW):
        scratch[lax.rem(me + ROW - o, ROW)] = arrays[o][...]


def spread_decays(blocks, y):
    rows = lax.broadcasted_iota(jnp.int32, (HEADS, PARTS * LANE), 0)
    cols = lax.broadcasted_iota(jnp.int32, (HEADS, PARTS * LANE), 1)
    pick = jnp.where(rows == y * (PARTS * 2) + (cols >> 6), 1.0, 0.0).astype(BF16)
    return jnp.dot(jnp.concatenate(blocks, axis=0), pick, preferred_element_type=F32)


def decay_of(wide, block, p, c):
    cols = slice(c * LANE, (c + 1) * LANE)
    return wide[block * NS + p : block * NS + p + 1, cols] + wide[block * NS + 2 + p : block * NS + 3 + p, cols]


def groups():
    return [(p, c, (p * PARTS + c) * NS) for p in range(2) for c in range(PARTS)]


def row_kernel(*refs):
    ins, out, scr = refs[:ROW], refs[ROW], refs[ROW + 1]
    y = lax.rem(lax.axis_index("seq"), ROW)
    place(ins, scr, y)
    wide = spread_decays([scr[b, STATE_ROWS:, :] for b in range(ROW)], y)
    for p, c, at in groups():
        state = jnp.zeros((NS, LANE), F32)
        for b in range(ROW):
            half = decay_of(wide, b, p, c)
            state = half * (half * state + scr[b, at : at + NS, :].astype(F32))
        out[at : at + NS, :] = state.astype(BF16)
    compact = [scr[b, STATE_ROWS:, :].astype(F32) for b in range(ROW)]
    row = lax.broadcasted_iota(jnp.int32, (NS, LANE), 0)
    dec = jnp.zeros((NS, LANE), F32)
    for p in range(2):
        all_rows = jnp.ones((1, LANE), F32)
        for b in range(ROW):
            half = compact[b][p : p + 1, :] + compact[b][2 + p : 3 + p, :]
            all_rows = all_rows * (half * half)
        high, low = halves(all_rows)
        dec = jnp.where(row == p, high.astype(F32), jnp.where(row == 2 + p, low.astype(F32), dec))
    out[STATE_ROWS:, :] = dec.astype(BF16)


def row_totals(blocks):
    return pl.pallas_call(
        row_kernel,
        out_shape=jax.ShapeDtypeStruct((STATE_ROWS + NS, LANE), BF16),
        in_specs=[VM] * ROW,
        out_specs=VM,
        scratch_shapes=[pltpu.VMEM((ROW, STATE_ROWS + NS, LANE), BF16)],
        cost_estimate=cost(1),
        compiler_params=params(),
        name="row_totals",
    )(*blocks)


def enter_kernel(group_ref, *refs):
    blocks, totals, outs = refs[:ROW], refs[ROW : 2 * ROW], refs[2 * ROW : 3 * ROW]
    scr, rows, start, stage = refs[3 * ROW :]
    me = lax.axis_index("seq")
    x, y = lax.div(me, ROW), lax.rem(me, ROW)
    place(blocks, scr, y)
    place(totals, rows, x)
    wide = spread_decays(
        [scr[b, STATE_ROWS:, :] for b in range(ROW)] + [rows[b, STATE_ROWS:, :] for b in range(ROW)], y
    )
    for p, c, at in groups():
        state = jnp.zeros((NS, LANE), F32)
        for b in range(ROW):
            start[b, at : at + NS, :] = state
            state = decay_of(wide, ROW + b, p, c) * state + rows[b, at : at + NS, :].astype(F32)
        start[ROW, at : at + NS, :] = state
    for p, c, at in groups():
        state = start[x, at : at + NS, :]
        for b in range(ROW):
            half = decay_of(wide, b, p, c)
            entering = half * state
            stage[b, at : at + NS, :] = entering.astype(BF16)
            state = half * (entering + scr[b, at : at + NS, :].astype(F32))
    second = group_ref[lax.axis_index("tp") * 2 + 1]
    for b in range(ROW):
        at = jnp.where(second == x * ROW + b, FINAL_ROWS, 0)
        final = start[ROW, pl.ds(pl.multiple_of(at, FINAL_ROWS), FINAL_ROWS), :]
        stage[b, STATE_ROWS:, :] = final.astype(BF16)
    for o in range(ROW):
        outs[o][...] = stage[lax.rem(y + o, ROW)]


def enter_states(group_of, blocks, totals):
    return pl.pallas_call(
        enter_kernel,
        out_shape=[jax.ShapeDtypeStruct((STATE_ROWS + FINAL_ROWS, LANE), BF16)] * ROW,
        in_specs=[SM] + [VM] * (2 * ROW),
        out_specs=[VM] * ROW,
        scratch_shapes=[
            pltpu.VMEM((ROW, STATE_ROWS + NS, LANE), BF16),
            pltpu.VMEM((ROW, STATE_ROWS + NS, LANE), BF16),
            pltpu.VMEM((ROW + 1, STATE_ROWS, LANE), F32),
            pltpu.VMEM((ROW, STATE_ROWS + FINAL_ROWS, LANE), BF16),
        ],
        cost_estimate=cost(2),
        compiler_params=params(),
        name="enter_states",
    )(group_of, *blocks, *totals)


def order_kernel(group_ref, pages, out):
    for r in range(SEQ):
        at = r % 2 * BLK
        out[group_ref[r]] = pages[r // 2, at : at + BLK, :]


def order_pages(group_of, pages):
    return pl.pallas_call(
        order_kernel,
        out_shape=jax.ShapeDtypeStruct((SEQ, BLK, 2 * HD), BF16),
        in_specs=[SM, VM],
        out_specs=VM,
        cost_estimate=cost(2),
        compiler_params=params(),
        name="order_pages",
    )(group_of, pages)


def spread(values, j, i):
    lanes = lax.broadcasted_iota(jnp.int32, values.shape, 1)
    return jnp.take_along_axis(values, j * (WC // HP) + 2 * i + (lanes >> 6), axis=1)


GATHERED = 8


def output_kernel(len_ref, x_hbm, dt_hbm, bc_hbm, rate_hbm, skip_hbm, *refs):
    enters, y_hbm, (after, ebig, both, mix, enter, x_buf, y_buf, dt_ref, bc_ref, rate_ref, skip_ref, c_rows, sem, out_sem) = (
        refs[:ROW],
        refs[ROW],
        refs[ROW + 1 :],
    )
    y = lax.rem(lax.axis_index("seq"), ROW)
    pairs = [(dt_hbm, dt_ref), (bc_hbm, bc_ref), (rate_hbm, rate_ref), (skip_hbm, skip_ref)]
    pairs += [(enters[o].at[pl.ds(0, STATE_ROWS), :], enter.at[lax.rem(y + ROW - o, ROW)]) for o in range(ROW)]
    small = fetch(pairs, sem, 2 * STEPS)
    for c in block_copies(x_hbm, x_buf, sem):
        c.start()
    spread_matrix(ebig)
    for c in small:
        c.wait()
    rows = lax.broadcasted_iota(jnp.int32, (BLK, BLK), 0)
    cols = lax.broadcasted_iota(jnp.int32, (BLK, BLK), 1)
    for p in range(2):
        live, step, rel, mid = decays(len_ref, dt_ref, rate_ref, p)
        after[p] = jnp.exp(rel) * live
        factors = [jnp.exp(-rel) * step, jnp.broadcast_to(skip_ref[...] * live, (NS, HEADS)), jnp.exp(rel) * live]
        for at, v in zip((0, BLK, BLK + NS), factors):
            high, low = halves(v)
            both[p, at : at + v.shape[0], :HEADS] = high
            both[p, at : at + v.shape[0], HEADS:] = low
        maps = jnp.transpose(bc_ref[p].astype(F32)).astype(BF16)
        c_rows[p] = maps[:, NS:]
        scores = jnp.dot(c_rows[p], bc_ref[p, :NS, :], preferred_element_type=F32)
        mix[p] = jnp.where(rows >= cols, scores, 0.0).astype(BF16)
    for p in range(2):

        def body(j, carry):
            block_copy(x_hbm, x_buf, sem, p, j).wait()
            at = pl.ds(pl.multiple_of(j * WC, WC), WC)
            ej = spread_rows(ebig, j)
            x = x_buf[p, :, at].astype(F32)
            factor = jnp.dot(both[p, : BLK + NS, :], ej, preferred_element_type=F32)
            xp = (x * factor[:BLK]).astype(BF16)
            first = (p * 2 + lax.rem(j, 2)) * CHUNKS * NS
            entering = enter[lax.div(j, 2), pl.ds(pl.multiple_of(first, CHUNKS * NS), CHUNKS * NS), :]
            entering = jnp.concatenate([entering[i * NS : (i + 1) * NS] for i in range(CHUNKS)], axis=1)
            total = jnp.dot(mix[p], xp, preferred_element_type=F32) + jnp.dot(
                c_rows[p], entering, preferred_element_type=F32
            )
            scales = [spread(after[p], j, i) for i in range(GATHERED)]
            if GATHERED < CHUNKS:
                scales.append(jnp.dot(both[p, BLK + NS :, :], ej[:, GATHERED * LANE :], preferred_element_type=F32))
            scale = jnp.concatenate(scales, axis=1)
            y_buf[p, :, at] = (scale * total + factor[BLK : BLK + 1] * x).astype(BF16)
            block_copy(y_hbm, y_buf, out_sem, p, j, out=True).start()
            return carry

        lax.fori_loop(0, STEPS, body, 0)
    for c in block_copies(y_hbm, y_buf, out_sem, out=True):
        c.wait()


def block_outputs(lengths, x_in, dt_raw, bc_in, rate, skip, entering):
    return pl.pallas_call(
        output_kernel,
        out_shape=jax.ShapeDtypeStruct((2, BLK, WIDTH), BF16),
        in_specs=[SM] + [ANY] * (5 + ROW),
        out_specs=ANY,
        scratch_shapes=[
            pltpu.VMEM((2, BLK, HEADS), F32),
            pltpu.VMEM((3 * HEADS, WC), BF16),
            pltpu.VMEM((2, 2 * BLK + NS, 2 * HEADS), BF16),
            pltpu.VMEM((2, BLK, BLK), BF16),
            pltpu.VMEM((ROW, STATE_ROWS, LANE), BF16),
            pltpu.VMEM((2, BLK, WIDTH), BF16),
            pltpu.VMEM((2, BLK, WIDTH), BF16),
            pltpu.VMEM((2, BLK, HEADS), BF16),
            pltpu.VMEM((2, 2 * NS, BLK), BF16),
            pltpu.VMEM((1, HEADS), F32),
            pltpu.VMEM((1, HEADS), F32),
            pltpu.VMEM((2, BLK, NS), BF16),
            pltpu.SemaphoreType.DMA((2 * STEPS + 4 + ROW,)),
            pltpu.SemaphoreType.DMA((2 * STEPS,)),
        ],
        cost_estimate=cost(12),
        compiler_params=params(60),
        name="block_outputs",
    )(lengths, x_in, dt_raw, bc_in, rate, skip, *entering)


def my_prompt(group_ref):
    mine = lax.axis_index("seq")
    prompt = jnp.int32(0)
    for r in range(SEQ):
        prompt = jnp.where(group_ref[r] == mine, r, prompt)
    return prompt


def attend_kernel(
    group_ref, len_ref, slot_ref, recv, q_ref, fresh_ref, pool, out_ref, zeros, sem
):
    prompt = my_prompt(group_ref)
    length = len_ref[prompt]
    zeros[...] = jnp.zeros(zeros.shape, BF16)

    def page_copy(s, live):
        at = pl.ds(pl.multiple_of(slot_ref[prompt, s] * BLK, BLK), BLK)
        source = recv.at[s] if live else zeros
        return pltpu.make_async_copy(source, pool.at[0, at, :], sem.at[s])

    for s in range(SEQ):

        @pl.when(length > s * BLK)
        def _():
            page_copy(s, True).start()

        @pl.when(length <= s * BLK)
        def _():
            page_copy(s, False).start()

    q = q_ref[0].astype(F32)
    q = jnp.concatenate([q[:, h * HD : (h + 1) * HD] for h in range(WC // HD)], axis=0).astype(BF16)
    fresh = fresh_ref[0].astype(F32)
    fresh = jnp.concatenate([fresh, jnp.zeros((12, 2 * HD), F32)], axis=0).astype(BF16)
    scale = HD**-0.5
    contract = (((1,), (1,)), ((), ()))
    rows = lax.broadcasted_iota(jnp.int32, (q.shape[0], fresh.shape[0]), 0)
    cols = lax.broadcasted_iota(jnp.int32, (q.shape[0], fresh.shape[0]), 1)
    new = lax.dot_general(q, fresh[:, :HD], contract, preferred_element_type=F32) * scale
    new = jnp.where(cols <= (rows & 3), new, -1e30)
    peak = jnp.max(new, axis=1, keepdims=True)
    old = []
    for s in range(SEQ):
        part = lax.dot_general(q, recv[s, :, :HD], contract, preferred_element_type=F32) * scale
        part = jnp.where(length > s * BLK, part, -1e30)
        old.append(part)
        peak = jnp.maximum(peak, jnp.max(part, axis=1, keepdims=True))
    prob = jnp.exp(new - peak)
    total = jnp.sum(prob, axis=1, keepdims=True)
    mixed = jnp.dot(prob.astype(BF16), fresh[:, HD:], preferred_element_type=F32)
    for s in range(SEQ):
        prob = jnp.exp(old[s] - peak)
        total = total + jnp.sum(prob, axis=1, keepdims=True)
        mixed = mixed + jnp.dot(prob.astype(BF16), recv[s, :, HD:], preferred_element_type=F32)
    result = mixed / total
    steps = out_ref.shape[1]
    for h in range(q.shape[0] // steps):
        out_ref[0, :, h * HD : (h + 1) * HD] = result[h * steps : (h + 1) * steps].astype(BF16)
    for s in range(SEQ):
        page_copy(s, True).wait()


def attend(group_of, lengths, slot_of, recv, queries, fresh):
    return pl.pallas_call(
        attend_kernel,
        out_shape=[
            jax.ShapeDtypeStruct((1, SEQ * BLK, 2 * HD), BF16),
            jax.ShapeDtypeStruct((1, 4, WC), BF16),
        ],
        in_specs=[SM, SM, SM, VM, VM, VM],
        out_specs=[ANY, VM],
        scratch_shapes=[pltpu.VMEM((BLK, 2 * HD), BF16), pltpu.SemaphoreType.DMA((SEQ,))],
        cost_estimate=cost(5),
        compiler_params=params(),
        name="attend",
    )(group_of, lengths, slot_of, recv, queries, fresh)


def decode_kernel(inputs, maps_ref, rate_ref, skip_ref, *refs):
    finals, (own, other, fin, res) = refs[:ROW], refs[ROW:]
    core = lax.rem(lax.axis_index("tp"), 2)
    y = lax.rem(lax.axis_index("seq"), ROW)
    for o in range(ROW):
        fin[lax.rem(y + ROW - o, ROW)] = finals[o][STATE_ROWS:, :]
    maps = maps_ref[0].astype(F32)
    eye = lax.broadcasted_iota(jnp.int32, (NS, NS), 0) == lax.broadcasted_iota(jnp.int32, (NS, NS), 1)

    def column(k, at):
        return jnp.sum(jnp.where(eye, maps[k : k + 1, at : at + NS], 0.0), axis=1, keepdims=True)

    b_cols = [column(k, 0) for k in range(4)]
    c_cols = [column(k, NS) for k in range(4)]
    heads = WC // HP
    rows = lax.broadcasted_iota(jnp.int32, (heads, WC), 0)
    cols = lax.broadcasted_iota(jnp.int32, (heads, WC), 1)
    spread = jnp.where(rows == (cols >> 6), 1.0, 0.0).astype(F32)
    raw = [inputs[t, DEC_X + 32 : DEC_X + 48, :].astype(F32)[:4, :heads] for t in range(TP)]
    step = softplus(jnp.concatenate(raw, axis=0))
    parts = [slice(t * heads, (t + 1) * heads) for t in range(TP)]
    rates = jnp.concatenate([jnp.broadcast_to(rate_ref[:, part], (4, heads)) for part in parts], axis=0)
    skips = jnp.concatenate([skip_ref[:, part] for part in parts], axis=0)
    small = jnp.concatenate([step, jnp.exp(-step * rates), skips], axis=0)
    wide = jnp.dot(small, spread, precision=highest, preferred_element_type=F32)

    def unfold(rows):
        return jnp.concatenate([rows[q * 4 : (q + 1) * 4] for q in range(4)], axis=1)

    sums = [jnp.zeros((1, 1), F32)] * 4
    for t in range(TP):
        x = unfold(inputs[t, DEC_X : DEC_X + 16, :].astype(F32))
        z = unfold(inputs[t, DEC_X + 16 : DEC_X + 32, :].astype(F32))
        gate = z / (1.0 + jnp.exp(-z))
        chunks = [t * CHUNKS + i for i in range(CHUNKS)]
        state = jnp.concatenate(
            [fin[k // PARTS, k % PARTS * NS : (k % PARTS + 1) * NS, :].astype(F32) for k in chunks], axis=1
        )
        skip = wide[8 * TP + t : 8 * TP + t + 1]
        for k in range(4):
            wide_step = wide[4 * t + k : 4 * t + k + 1]
            fade = wide[4 * TP + 4 * t + k : 4 * TP + 4 * t + k + 1]
            state = fade * state + b_cols[k] * (wide_step * x[k : k + 1])
            read = jnp.sum(c_cols[k] * state, axis=0, keepdims=True) + skip * x[k : k + 1]
            v = read * gate[k : k + 1]
            res[t, NS + k : NS + k + 1, :] = v
            sums[k] = sums[k] + jnp.sum(v * v, axis=1, keepdims=True)
        res[t, :NS, :] = state
    factor = jnp.concatenate([lax.rsqrt(sums[k] / WIDTH + 1e-05) for k in range(4)], axis=0)
    for t in range(TP):
        res[t, NS : NS + 4, :] = res[t, NS : NS + 4, :] * factor
        res[t, NS + 4 :, :] = jnp.zeros((4, WC), F32)
    for z in range(ROW):
        own[z] = res[2 * z + core]
        other[z] = res[2 * z + 1 - core]


def decode(inputs, maps, rate, skip, finals):
    return pl.pallas_call(
        decode_kernel,
        out_shape=[jax.ShapeDtypeStruct((ROW, NS + 8, WC), F32)] * 2,
        in_specs=[VM] * (4 + ROW),
        out_specs=[VM] * 2,
        scratch_shapes=[
            pltpu.VMEM((ROW, FINAL_ROWS, LANE), BF16),
            pltpu.VMEM((TP, NS + 8, WC), F32),
        ],
        cost_estimate=cost(4),
        compiler_params=params(),
        name="decode",
    )(inputs, maps, rate, skip, *finals)


def side_kernel(group_ref, own, other, *outs):
    me = lax.axis_index("tp")
    z, core = lax.div(me, 2), lax.rem(me, 2)
    mine = lax.rem(lax.div(my_prompt(group_ref), 2), 2) == core
    for o in range(ROW):
        at = lax.rem(z + o, ROW)
        outs[o][...] = jnp.where(mine, own[at], other[at])


def choose_side(group_of, own, other):
    return pl.pallas_call(
        side_kernel,
        out_shape=[jax.ShapeDtypeStruct((NS + 8, WC), F32)] * ROW,
        in_specs=[SM, VM, VM],
        out_specs=[VM] * ROW,
        cost_estimate=cost(1),
        compiler_params=params(),
        name="choose_side",
    )(group_of, own, other)


def pick_kernel(group_ref, gain_ref, *refs):
    results, (state_ref, out_ref) = refs[:ROW], refs[ROW:]
    holder = lax.div(my_prompt(group_ref), 4)
    distance = lax.rem(lax.div(lax.axis_index("tp"), 2) + ROW - holder, ROW)
    for o in range(ROW):

        @pl.when(distance == o)
        def _():
            state_ref[0] = results[o][:NS, :]
            out_ref[0] = (results[o][NS : NS + 4, :] * gain_ref[...].astype(F32)).astype(BF16)


def pick(group_of, gain, results):
    return pl.pallas_call(
        pick_kernel,
        out_shape=[
            jax.ShapeDtypeStruct((1, NS, WC), F32),
            jax.ShapeDtypeStruct((1, 4, WC), BF16),
        ],
        in_specs=[SM] + [VM] * (1 + ROW),
        out_specs=[VM] * 2,
        cost_estimate=cost(1),
        compiler_params=params(),
        name="pick",
    )(group_of, gain, *results)


def along_z(arrays):
    moves = [[(i, (i + 2 * o) % TP) for i in range(TP)] for o in range(ROW)]
    return [arrays[0]] + [lax.ppermute(arrays[o], "tp", moves[o]) for o in range(1, ROW)]


def along_y(arrays):
    moves = [[(x * ROW + y, x * ROW + (y + o) % ROW) for x in range(ROW) for y in range(ROW)] for o in range(ROW)]
    return [arrays[0]] + [lax.ppermute(arrays[o], "seq", moves[o]) for o in range(1, ROW)]


def along_x(arrays):
    moves = [[(i, (i + o * ROW) % SEQ) for i in range(SEQ)] for o in range(ROW)]
    return [arrays[0]] + [lax.ppermute(arrays[o], "seq", moves[o]) for o in range(1, ROW)]


def shards(
    x_in, dt_raw, bc_in, decay_rate, skip_gain, kv_pre, lengths, group_of, slot_of,
    dec_x, dec_dt, dec_bc, dec_z, norm_gain, dec_q, dec_kv,
):
    rate = decay_rate.reshape(1, HEADS)
    skip = skip_gain.reshape(1, HEADS)
    gain = norm_gain.reshape(1, -1)
    maps = jnp.swapaxes(bc_in, 1, 2)

    *local, sent = local_states(lengths, x_in, dt_raw, maps, rate, kv_pre, dec_x, dec_z, dec_dt)
    pages = lax.all_to_all(sent, "tp", split_axis=0, concat_axis=0, tiled=True)
    blocks = along_y(local)
    totals = along_x([row_totals(blocks)] * ROW)
    pages, unused = lax.optimization_barrier((pages, totals))
    entering = along_y(enter_states(group_of, blocks, totals))
    ordered, entering = lax.optimization_barrier((order_pages(group_of, pages), entering))
    recv = lax.all_to_all(ordered, "seq", split_axis=0, concat_axis=0, tiled=True)
    own, other = decode(pages, dec_bc, rate, skip, entering)
    other = lax.ppermute(other, "tp", [(i, i ^ 1) for i in range(TP)])
    results = along_z(choose_side(group_of, own, other))
    dec_state, dec_mamba = pick(group_of, gain, results)
    y_pre = block_outputs(lengths, x_in, dt_raw, maps, rate, skip, entering)
    kv_pool, dec_attn = attend(group_of, lengths, slot_of, recv, dec_q, dec_kv)
    return (y_pre, kv_pool, dec_mamba, dec_state, dec_attn)


def solution(mesh):
    return jax.shard_map(
        shards,
        mesh=mesh,
        in_specs=(
            P("tp", "seq", None),
            P("tp", "seq", None),
            P("tp", "seq", None),
            P(),
            P(),
            P("tp", "seq", None),
            P(),
            P(),
            P(),
            P("seq", None, "tp"),
            P("seq", None, "tp"),
            P("seq", None, None),
            P("seq", None, "tp"),
            P("tp"),
            P("seq", None, "tp"),
            P("seq", None, "tp"),
        ),
        out_specs=(
            P("tp", "seq", None),
            P("seq", None, "tp"),
            P("seq", None, "tp"),
            P("seq", None, "tp"),
            P("seq", None, "tp"),
        ),
        check_vma=False,
    )
```

```python
import jax
import jax.numpy as jnp
from jax import lax
from jax.experimental import pallas as pl
from jax.experimental.pallas import tpu as pltpu
from jax.sharding import PartitionSpec as P

HD = 128
BLK = 256
HP = 64
NS = 16
HEADS = 128
WIDTH = 8192
SEQ = 16
TP = 8
WC = 1024
LANE = 128
CHUNKS = WC // LANE
STEPS = WIDTH // WC
ROW = 4
PARTS = WIDTH // (ROW * LANE)
STATE_ROWS = 2 * PARTS * NS
FINAL_ROWS = PARTS * NS
DEC_X = 2 * BLK
PAGE_ROWS = 2 * BLK + 48
F32 = jnp.float32
BF16 = jnp.bfloat16
MIB = 1024 * 1024
KV_PARTS = 2
highest = lax.Precision.HIGHEST
ANY = pl.BlockSpec(memory_space=pl.ANY)
VM = pl.BlockSpec(memory_space=pltpu.VMEM)
SM = pl.BlockSpec(memory_space=pltpu.SMEM)


def params(mib=44):
    return pltpu.CompilerParams(vmem_limit_bytes=mib * MIB)


def cost(us):
    return pl.CostEstimate(flops=0, bytes_accessed=int(us * 3.0e6), transcendentals=0)


def softplus(v):
    return jnp.maximum(v, 0.0) + jnp.log1p(jnp.exp(-jnp.abs(v)))


def halves(v):
    high = v.astype(BF16)
    return high, (v - high.astype(F32)).astype(BF16)


def fetch(pairs, sem, first=0):
    copies = [pltpu.make_async_copy(src, dst, sem.at[first + n]) for n, (src, dst) in enumerate(pairs)]
    for c in copies:
        c.start()
    return copies


def split_start(kv, x_hbm, z_hbm, dt_hbm, out, buf, x_buf, z_buf, dt_buf, rows, sem, out_sem):
    small = fetch([(x_hbm.at[0], x_buf), (z_hbm.at[0], z_buf), (dt_hbm.at[0], dt_buf)], sem, 2 * TP)
    parts = [(i, pl.ds(q * BLK // KV_PARTS, BLK // KV_PARTS)) for i in range(2) for q in range(KV_PARTS)]
    arrive = fetch([(kv.at[part], buf.at[part]) for part in parts], sem)

    def fold(part):
        part = part.astype(F32)
        return jnp.concatenate([part[:, q * 256 : (q + 1) * 256] for q in range(4)], axis=0)

    def finish():
        for c in small:
            c.wait()
        rows[:16, :] = fold(x_buf[...]).astype(BF16)
        rows[16:32, :] = fold(z_buf[...]).astype(BF16)
        steps = dt_buf[...].astype(F32)
        steps = jnp.concatenate([steps, jnp.zeros((steps.shape[0], 256 - steps.shape[1]), F32)], axis=1)
        steps = jnp.concatenate([steps, jnp.zeros((12, 256), F32)], axis=0)
        rows[32:, :] = steps.astype(BF16)
        leave = fetch([(rows, out.at[h, pl.ds(DEC_X, 48), :]) for h in range(TP)], out_sem)
        for i in range(2):
            for c in arrive[KV_PARTS * i : KV_PARTS * (i + 1)]:
                c.wait()
            heads = [(h, pl.ds(h * 2 * HD, 2 * HD)) for h in range(TP)]
            leave += fetch(
                [(buf.at[i, :, cols], out.at[h, pl.ds(i * BLK, BLK), :]) for h, cols in heads], out_sem, TP * (1 + i)
            )
        return leave

    return finish


def spread_matrix(ebig):
    rows = lax.broadcasted_iota(jnp.int32, ebig.shape, 0)
    cols = lax.broadcasted_iota(jnp.int32, ebig.shape, 1)
    ebig[...] = jnp.where((rows & (HEADS - 1)) == (cols >> 6), 1.0, 0.0).astype(BF16)


def spread_rows(ebig, j):
    start = pl.multiple_of(HEADS - (WC // HP) * j, 16)
    return ebig[pl.ds(start, 2 * HEADS), :]


def decays(len_ref, dt_ref, rate_ref, p):
    prompt = lax.axis_index("tp") * 2 + p
    live = jnp.where(len_ref[prompt] > lax.axis_index("seq") * BLK, 1.0, 0.0).astype(F32)
    step = softplus(dt_ref[p].astype(F32)) * live
    rows = lax.broadcasted_iota(jnp.int32, (BLK, BLK), 0)
    cols = lax.broadcasted_iota(jnp.int32, (BLK, BLK), 1)
    tri = jnp.where(rows >= cols, 1.0, 0.0).astype(F32)
    cum = jnp.dot(tri, -step * rate_ref[...], precision=highest, preferred_element_type=F32)
    mid = 0.5 * cum[BLK - 1 :, :]
    return live, step, cum - mid, mid


def block_copies(hbm, buf, sem, out=False):
    copies = []
    for p in range(2):
        for j in range(STEPS):
            cols = pl.ds(j * WC, WC)
            ends = (hbm.at[p, :, cols], buf.at[p, :, cols])
            copies.append(pltpu.make_async_copy(*(ends[::-1] if out else ends), sem.at[p * STEPS + j]))
    return copies


def block_copy(hbm, buf, sem, p, j, out=False):
    cols = pl.ds(pl.multiple_of(j * WC, WC), WC)
    ends = (hbm.at[p, :, cols], buf.at[p, :, cols])
    return pltpu.make_async_copy(*(ends[::-1] if out else ends), sem.at[p * STEPS + j])


def local_kernel(len_ref, x_hbm, dt_hbm, bc_hbm, rate_hbm, kv, dx_hbm, dz_hbm, ddt_hbm, *refs):
    outs, split, (stage, ft, bt, x_buf, dt_ref, bc_ref, rate_ref, sem), rest = (
        refs[:ROW],
        refs[ROW],
        refs[ROW + 1 : ROW + 9],
        refs[ROW + 9 :],
    )
    small = fetch([(dt_hbm, dt_ref), (bc_hbm, bc_ref), (rate_hbm, rate_ref)], sem, 2 * STEPS)
    x_copies = block_copies(x_hbm, x_buf, sem)
    for c in x_copies[:STEPS]:
        c.start()
    finish = split_start(kv, dx_hbm, dz_hbm, ddt_hbm, split, *rest)
    for c in x_copies[STEPS:]:
        c.start()
    for c in small:
        c.wait()
    lane = lax.broadcasted_iota(jnp.int32, (NS, LANE), 1)
    row = lax.broadcasted_iota(jnp.int32, (NS, HEADS), 0)
    heads = WC // HP
    dec = jnp.zeros((NS, HEADS), F32)
    for p in range(2):
        live, step, rel, mid = decays(len_ref, dt_ref, rate_ref, p)
        ft[p] = jnp.transpose(jnp.exp(-rel) * step)
        bt[p] = bc_ref[p, :NS, :].astype(F32)
        high, low = halves(jnp.exp(mid))
        dec = jnp.where(row == p, high.astype(F32), jnp.where(row == 2 + p, low.astype(F32), dec))
    for s in range(ROW):
        stage[s, STATE_ROWS:, :] = dec.astype(BF16)
    for p in range(2):
        if p == 1:
            leave = finish()

        def body(j, carry):
            quarter, part = lax.div(j, 2), lax.rem(j, 2)
            block_copy(x_hbm, x_buf, sem, p, j).wait()
            fj = ft[p, pl.ds(pl.multiple_of(j * heads, heads), heads), :]
            for u in range(WC // 256):
                left = jnp.concatenate([bt[p] * fj[u * 4 + h : u * 4 + h + 1, :] for h in range(4)], axis=0)
                cols = pl.ds(pl.multiple_of(j * WC + u * 256, 256), 256)
                prod = jnp.dot(left.astype(BF16), x_buf[p, :, cols], preferred_element_type=F32)
                for v in range(2):
                    cols = slice(v * LANE, (v + 1) * LANE)
                    first = prod[2 * v * NS : (2 * v + 1) * NS, cols]
                    second = prod[(2 * v + 1) * NS : (2 * v + 2) * NS, cols]
                    local = jnp.where(lane < HP, first, second).astype(BF16)
                    at = ((p * 2 + part) * CHUNKS + u * 2 + v) * NS
                    stage[quarter, pl.ds(pl.multiple_of(at, NS), NS), :] = local
            return carry

        lax.fori_loop(0, STEPS, body, 0)
    y = lax.rem(lax.axis_index("seq"), ROW)
    leave += fetch([(stage.at[lax.rem(y + o, ROW)], outs[o]) for o in range(ROW)], sem, 2 * STEPS)
    for c in leave:
        c.wait()


def local_states(lengths, x_in, dt_raw, bc_in, rate, kv_pre, dec_x, dec_z, dec_dt):
    return pl.pallas_call(
        local_kernel,
        out_shape=[jax.ShapeDtypeStruct((STATE_ROWS + NS, LANE), BF16)] * ROW
        + [jax.ShapeDtypeStruct((TP, PAGE_ROWS, 2 * HD), BF16)],
        in_specs=[SM] + [ANY] * 8,
        out_specs=[ANY] * (ROW + 1),
        scratch_shapes=[
            pltpu.VMEM((ROW, STATE_ROWS + NS, LANE), BF16),
            pltpu.VMEM((2, HEADS, BLK), F32),
            pltpu.VMEM((2, NS, BLK), F32),
            pltpu.VMEM((2, BLK, WIDTH), BF16),
            pltpu.VMEM((2, BLK, HEADS), BF16),
            pltpu.VMEM((2, 2 * NS, BLK), BF16),
            pltpu.VMEM((1, HEADS), F32),
            pltpu.SemaphoreType.DMA((2 * STEPS + ROW,)),
            pltpu.VMEM((2, BLK, TP * 2 * HD), BF16),
            pltpu.VMEM((4, WC), BF16),
            pltpu.VMEM((4, WC), BF16),
            pltpu.VMEM((4, WC // HP), BF16),
            pltpu.VMEM((48, 2 * HD), BF16),
            pltpu.SemaphoreType.DMA((2 * TP + 3,)),
            pltpu.SemaphoreType.DMA((3 * TP,)),
        ],
        cost_estimate=cost(6),
        compiler_params=params(60),
        name="local_states",
    )(lengths, x_in, dt_raw, bc_in, rate, kv_pre, dec_x, dec_z, dec_dt)


def place(arrays, scratch, me):
    for o in range(ROW):
        scratch[lax.rem(me + ROW - o, ROW)] = arrays[o][...]


def spread_decays(blocks, y):
    rows = lax.broadcasted_iota(jnp.int32, (HEADS, PARTS * LANE), 0)
    cols = lax.broadcasted_iota(jnp.int32, (HEADS, PARTS * LANE), 1)
    pick = jnp.where(rows == y * (PARTS * 2) + (cols >> 6), 1.0, 0.0).astype(BF16)
    return jnp.dot(jnp.concatenate(blocks, axis=0), pick, preferred_element_type=F32)


def decay_of(wide, block, p, c):
    cols = slice(c * LANE, (c + 1) * LANE)
    return wide[block * NS + p : block * NS + p + 1, cols] + wide[block * NS + 2 + p : block * NS + 3 + p, cols]


def groups():
    return [(p, c, (p * PARTS + c) * NS) for p in range(2) for c in range(PARTS)]


def row_kernel(*refs):
    ins, out, scr = refs[:ROW], refs[ROW], refs[ROW + 1]
    y = lax.rem(lax.axis_index("seq"), ROW)
    place(ins, scr, y)
    wide = spread_decays([scr[b, STATE_ROWS:, :] for b in range(ROW)], y)
    for p, c, at in groups():
        state = jnp.zeros((NS, LANE), F32)
        for b in range(ROW):
            half = decay_of(wide, b, p, c)
            state = half * (half * state + scr[b, at : at + NS, :].astype(F32))
        out[at : at + NS, :] = state.astype(BF16)
    once = [scr[b, STATE_ROWS:, :].astype(F32) for b in range(ROW)]
    out[STATE_ROWS:, :] = compact_decays(once + once)


def row_totals(blocks):
    return pl.pallas_call(
        row_kernel,
        out_shape=jax.ShapeDtypeStruct((STATE_ROWS + NS, LANE), BF16),
        in_specs=[VM] * ROW,
        out_specs=VM,
        scratch_shapes=[pltpu.VMEM((ROW, STATE_ROWS + NS, LANE), BF16)],
        cost_estimate=cost(1),
        compiler_params=params(),
        name="row_totals",
    )(*blocks)


def compact_decays(parts):
    row = lax.broadcasted_iota(jnp.int32, (NS, LANE), 0)
    dec = jnp.zeros((NS, LANE), F32)
    for p in range(2):
        product = jnp.ones((1, LANE), F32)
        for part in parts:
            product = product * (part[p : p + 1, :] + part[2 + p : 3 + p, :])
        high, low = halves(product)
        dec = jnp.where(row == p, high.astype(F32), jnp.where(row == 2 + p, low.astype(F32), dec))
    return dec.astype(BF16)


def place_pair(own, near, scratch, x):
    scratch[lax.rem(x, 2)] = own[...]
    scratch[1 - lax.rem(x, 2)] = near[...]


def pair_kernel(own, near, out, rows):
    me = lax.axis_index("seq")
    x, y = lax.div(me, ROW), lax.rem(me, ROW)
    place_pair(own, near, rows, x)
    wide = spread_decays([rows[1, STATE_ROWS:, :]], y)
    for p, c, at in groups():
        first, second = (rows[b, at : at + NS, :].astype(F32) for b in range(2))
        out[at : at + NS, :] = (decay_of(wide, 0, p, c) * first + second).astype(BF16)
    out[STATE_ROWS:, :] = compact_decays([rows[b, STATE_ROWS:, :].astype(F32) for b in range(2)])


def pair_totals(own, near):
    return pl.pallas_call(
        pair_kernel,
        out_shape=jax.ShapeDtypeStruct((STATE_ROWS + NS, LANE), BF16),
        in_specs=[VM] * 2,
        out_specs=VM,
        scratch_shapes=[pltpu.VMEM((2, STATE_ROWS + NS, LANE), BF16)],
        cost_estimate=cost(1),
        compiler_params=params(),
        name="pair_totals",
    )(own, near)


def enter_kernel(group_ref, own, near, far, *refs):
    blocks, outs = refs[:ROW], refs[ROW : 2 * ROW]
    scr, rows, final, stage = refs[2 * ROW :]
    me = lax.axis_index("seq")
    x, y = lax.div(me, ROW), lax.rem(me, ROW)
    place(blocks, scr, y)
    place_pair(own, near, rows, x)
    ends = [rows[0, STATE_ROWS:, :], rows[1, STATE_ROWS:, :], far[STATE_ROWS:, :]]
    wide = spread_decays([scr[b, STATE_ROWS:, :] for b in range(ROW)] + ends + ends[:1], y)
    late, odd = x >= 2, lax.rem(x, 2) == 1
    for p, c, at in groups():
        first, second = (rows[b, at : at + NS, :].astype(F32) for b in range(2))
        other = far[at : at + NS, :].astype(F32)
        before = jnp.where(late, other, 0.0)
        middle = decay_of(wide, ROW, p, c) * before + first
        after = decay_of(wide, ROW + 1, p, c) * middle + second
        final[at : at + NS, :] = jnp.where(late, after, decay_of(wide, ROW + 2, p, c) * after + other)
        state = jnp.where(odd, middle, before)
        for b in range(ROW):
            half = decay_of(wide, b, p, c)
            entering = half * state
            stage[b, at : at + NS, :] = entering.astype(BF16)
            state = half * (entering + scr[b, at : at + NS, :].astype(F32))
    second = group_ref[lax.axis_index("tp") * 2 + 1]
    for b in range(ROW):
        at = jnp.where(second == x * ROW + b, FINAL_ROWS, 0)
        chosen = final[pl.ds(pl.multiple_of(at, FINAL_ROWS), FINAL_ROWS), :]
        stage[b, STATE_ROWS:, :] = chosen.astype(BF16)
    for o in range(ROW):
        outs[o][...] = stage[lax.rem(y + o, ROW)]


def enter_states(group_of, own, near, far, blocks):
    return pl.pallas_call(
        enter_kernel,
        out_shape=[jax.ShapeDtypeStruct((STATE_ROWS + FINAL_ROWS, LANE), BF16)] * ROW,
        in_specs=[SM] + [VM] * (3 + ROW),
        out_specs=[VM] * ROW,
        scratch_shapes=[
            pltpu.VMEM((ROW, STATE_ROWS + NS, LANE), BF16),
            pltpu.VMEM((2, STATE_ROWS + NS, LANE), BF16),
            pltpu.VMEM((STATE_ROWS, LANE), F32),
            pltpu.VMEM((ROW, STATE_ROWS + FINAL_ROWS, LANE), BF16),
        ],
        cost_estimate=cost(2),
        compiler_params=params(),
        name="enter_states",
    )(group_of, own, near, far, *blocks)


def order_kernel(group_ref, pages, out):
    for r in range(SEQ):
        at = r % 2 * BLK
        out[group_ref[r]] = pages[r // 2, at : at + BLK, :]


def order_pages(group_of, pages):
    return pl.pallas_call(
        order_kernel,
        out_shape=jax.ShapeDtypeStruct((SEQ, BLK, 2 * HD), BF16),
        in_specs=[SM, VM],
        out_specs=VM,
        cost_estimate=cost(2),
        compiler_params=params(),
        name="order_pages",
    )(group_of, pages)


def spread(values, j, i):
    lanes = lax.broadcasted_iota(jnp.int32, values.shape, 1)
    return jnp.take_along_axis(values, j * (WC // HP) + 2 * i + (lanes >> 6), axis=1)


GATHERED = 8


def output_kernel(len_ref, x_hbm, dt_hbm, bc_hbm, rate_hbm, skip_hbm, *refs):
    enters, y_hbm, (after, ebig, both, mix, enter, x_buf, y_buf, dt_ref, bc_ref, rate_ref, skip_ref, c_rows, sem, out_sem) = (
        refs[:ROW],
        refs[ROW],
        refs[ROW + 1 :],
    )
    y = lax.rem(lax.axis_index("seq"), ROW)
    pairs = [(dt_hbm, dt_ref), (bc_hbm, bc_ref), (rate_hbm, rate_ref), (skip_hbm, skip_ref)]
    pairs += [(enters[o].at[pl.ds(0, STATE_ROWS), :], enter.at[lax.rem(y + ROW - o, ROW)]) for o in range(ROW)]
    small = fetch(pairs, sem, 2 * STEPS)
    for c in block_copies(x_hbm, x_buf, sem):
        c.start()
    spread_matrix(ebig)
    for c in small:
        c.wait()
    rows = lax.broadcasted_iota(jnp.int32, (BLK, BLK), 0)
    cols = lax.broadcasted_iota(jnp.int32, (BLK, BLK), 1)
    for p in range(2):
        live, step, rel, mid = decays(len_ref, dt_ref, rate_ref, p)
        after[p] = jnp.exp(rel) * live
        factors = [jnp.exp(-rel) * step, jnp.broadcast_to(skip_ref[...] * live, (NS, HEADS)), jnp.exp(rel) * live]
        for at, v in zip((0, BLK, BLK + NS), factors):
            high, low = halves(v)
            both[p, at : at + v.shape[0], :HEADS] = high
            both[p, at : at + v.shape[0], HEADS:] = low
        maps = jnp.transpose(bc_ref[p].astype(F32)).astype(BF16)
        c_rows[p] = maps[:, NS:]
        scores = jnp.dot(c_rows[p], bc_ref[p, :NS, :], preferred_element_type=F32)
        mix[p] = jnp.where(rows >= cols, scores, 0.0).astype(BF16)
    for p in range(2):

        def body(j, carry):
            block_copy(x_hbm, x_buf, sem, p, j).wait()
            at = pl.ds(pl.multiple_of(j * WC, WC), WC)
            ej = spread_rows(ebig, j)
            x = x_buf[p, :, at].astype(F32)
            factor = jnp.dot(both[p, : BLK + NS, :], ej, preferred_element_type=F32)
            xp = (x * factor[:BLK]).astype(BF16)
            first = (p * 2 + lax.rem(j, 2)) * CHUNKS * NS
            entering = enter[lax.div(j, 2), pl.ds(pl.multiple_of(first, CHUNKS * NS), CHUNKS * NS), :]
            entering = jnp.concatenate([entering[i * NS : (i + 1) * NS] for i in range(CHUNKS)], axis=1)
            total = jnp.dot(mix[p], xp, preferred_element_type=F32) + jnp.dot(
                c_rows[p], entering, preferred_element_type=F32
            )
            scales = [spread(after[p], j, i) for i in range(GATHERED)]
            if GATHERED < CHUNKS:
                scales.append(jnp.dot(both[p, BLK + NS :, :], ej[:, GATHERED * LANE :], preferred_element_type=F32))
            scale = jnp.concatenate(scales, axis=1)
            y_buf[p, :, at] = (scale * total + factor[BLK : BLK + 1] * x).astype(BF16)
            block_copy(y_hbm, y_buf, out_sem, p, j, out=True).start()
            return carry

        lax.fori_loop(0, STEPS, body, 0)
    for c in block_copies(y_hbm, y_buf, out_sem, out=True):
        c.wait()


def block_outputs(lengths, x_in, dt_raw, bc_in, rate, skip, entering):
    return pl.pallas_call(
        output_kernel,
        out_shape=jax.ShapeDtypeStruct((2, BLK, WIDTH), BF16),
        in_specs=[SM] + [ANY] * (5 + ROW),
        out_specs=ANY,
        scratch_shapes=[
            pltpu.VMEM((2, BLK, HEADS), F32),
            pltpu.VMEM((3 * HEADS, WC), BF16),
            pltpu.VMEM((2, 2 * BLK + NS, 2 * HEADS), BF16),
            pltpu.VMEM((2, BLK, BLK), BF16),
            pltpu.VMEM((ROW, STATE_ROWS, LANE), BF16),
            pltpu.VMEM((2, BLK, WIDTH), BF16),
            pltpu.VMEM((2, BLK, WIDTH), BF16),
            pltpu.VMEM((2, BLK, HEADS), BF16),
            pltpu.VMEM((2, 2 * NS, BLK), BF16),
            pltpu.VMEM((1, HEADS), F32),
            pltpu.VMEM((1, HEADS), F32),
            pltpu.VMEM((2, BLK, NS), BF16),
            pltpu.SemaphoreType.DMA((2 * STEPS + 4 + ROW,)),
            pltpu.SemaphoreType.DMA((2 * STEPS,)),
        ],
        cost_estimate=cost(12),
        compiler_params=params(54),
        name="block_outputs",
    )(lengths, x_in, dt_raw, bc_in, rate, skip, *entering)


def my_prompt(group_ref):
    mine = lax.axis_index("seq")
    prompt = jnp.int32(0)
    for r in range(SEQ):
        prompt = jnp.where(group_ref[r] == mine, r, prompt)
    return prompt


def attend_kernel(
    table, recv, q_ref, fresh_ref, gain_ref, *refs
):
    results, (pool, *outs), scratch = refs[:ROW], refs[ROW : ROW + 4], refs[ROW + 4 :]
    zeros, best, out_ref, mamba_ref, out_sem, sem = scratch
    prompt = my_prompt(table)
    length = table[SEQ + prompt]
    distance = lax.rem(lax.div(lax.axis_index("tp"), 2) + ROW - lax.div(prompt, 4), ROW)
    for o in range(ROW):

        @pl.when(distance == o)
        def _():
            best[...] = results[o][...]

    mamba_ref[0] = (best[NS : NS + 4, :] * gain_ref[...].astype(F32)).astype(BF16)
    ends = fetch([(best.at[pl.ds(0, NS), :], outs[1].at[0]), (mamba_ref, outs[2])], out_sem)
    zeros[...] = jnp.zeros(zeros.shape, BF16)

    def page_copy(s, live):
        at = pl.ds(pl.multiple_of(table[(2 + prompt) * SEQ + s] * BLK, BLK), BLK)
        source = recv.at[s] if live else zeros
        return pltpu.make_async_copy(source, pool.at[0, at, :], sem.at[s])

    for s in range(SEQ):

        @pl.when(length > s * BLK)
        def _():
            page_copy(s, True).start()

        @pl.when(length <= s * BLK)
        def _():
            page_copy(s, False).start()

    q = q_ref[0].astype(F32)
    q = jnp.concatenate([q[:, h * HD : (h + 1) * HD] for h in range(WC // HD)], axis=0).astype(BF16)
    fresh = fresh_ref[0].astype(F32)
    fresh = jnp.concatenate([fresh, jnp.zeros((12, 2 * HD), F32)], axis=0).astype(BF16)
    scale = HD**-0.5
    contract = (((1,), (1,)), ((), ()))
    rows = lax.broadcasted_iota(jnp.int32, (q.shape[0], fresh.shape[0]), 0)
    cols = lax.broadcasted_iota(jnp.int32, (q.shape[0], fresh.shape[0]), 1)
    new = lax.dot_general(q, fresh[:, :HD], contract, preferred_element_type=F32) * scale
    new = jnp.where(cols <= (rows & 3), new, -1e30)
    peak = jnp.max(new, axis=1, keepdims=True)
    old = []
    for s in range(SEQ):
        part = lax.dot_general(q, recv[s, :, :HD], contract, preferred_element_type=F32) * scale
        part = jnp.where(length > s * BLK, part, -1e30)
        old.append(part)
        peak = jnp.maximum(peak, jnp.max(part, axis=1, keepdims=True))
    prob = jnp.exp(new - peak)
    total = jnp.sum(prob, axis=1, keepdims=True)
    mixed = jnp.dot(prob.astype(BF16), fresh[:, HD:], preferred_element_type=F32)
    for s in range(SEQ):
        prob = jnp.exp(old[s] - peak)
        total = total + jnp.sum(prob, axis=1, keepdims=True)
        mixed = mixed + jnp.dot(prob.astype(BF16), recv[s, :, HD:], preferred_element_type=F32)
    result = mixed / total
    steps = out_ref.shape[1]
    for h in range(q.shape[0] // steps):
        out_ref[0, :, h * HD : (h + 1) * HD] = result[h * steps : (h + 1) * steps].astype(BF16)
    ends += fetch([(out_ref, outs[0])], out_sem, 2)
    for s in range(SEQ):
        page_copy(s, True).wait()
    for c in ends:
        c.wait()


def attend(table, recv, queries, fresh, gain, results):
    return pl.pallas_call(
        attend_kernel,
        out_shape=[
            jax.ShapeDtypeStruct((1, SEQ * BLK, 2 * HD), BF16),
            jax.ShapeDtypeStruct((1, 4, WC), BF16),
            jax.ShapeDtypeStruct((1, NS, WC), F32),
            jax.ShapeDtypeStruct((1, 4, WC), BF16),
        ],
        in_specs=[SM] + [VM] * (4 + ROW),
        out_specs=[ANY] * 4,
        scratch_shapes=[
            pltpu.VMEM((BLK, 2 * HD), BF16),
            pltpu.VMEM((NS + 8, WC), F32),
            pltpu.VMEM((1, 4, WC), BF16),
            pltpu.VMEM((1, 4, WC), BF16),
            pltpu.SemaphoreType.DMA((3,)),
            pltpu.SemaphoreType.DMA((SEQ,)),
        ],
        cost_estimate=cost(5),
        compiler_params=params(54),
        name="attend",
    )(table, recv, queries, fresh, gain, *results)


def decode_kernel(inputs, maps_ref, rate_ref, skip_ref, *refs):
    finals, (own, other, fin, res) = refs[:ROW], refs[ROW:]
    core = lax.rem(lax.axis_index("tp"), 2)
    y = lax.rem(lax.axis_index("seq"), ROW)
    for o in range(ROW):
        fin[lax.rem(y + ROW - o, ROW)] = finals[o][STATE_ROWS:, :]
    maps = maps_ref[0].astype(F32)
    eye = lax.broadcasted_iota(jnp.int32, (NS, NS), 0) == lax.broadcasted_iota(jnp.int32, (NS, NS), 1)

    def column(k, at):
        return jnp.sum(jnp.where(eye, maps[k : k + 1, at : at + NS], 0.0), axis=1, keepdims=True)

    b_cols = [column(k, 0) for k in range(4)]
    c_cols = [column(k, NS) for k in range(4)]
    heads = WC // HP
    rows = lax.broadcasted_iota(jnp.int32, (heads, WC), 0)
    cols = lax.broadcasted_iota(jnp.int32, (heads, WC), 1)
    spread = jnp.where(rows == (cols >> 6), 1.0, 0.0).astype(F32)
    raw = [inputs[t, DEC_X + 32 : DEC_X + 48, :].astype(F32)[:4, :heads] for t in range(TP)]
    step = softplus(jnp.concatenate(raw, axis=0))
    parts = [slice(t * heads, (t + 1) * heads) for t in range(TP)]
    rates = jnp.concatenate([jnp.broadcast_to(rate_ref[:, part], (4, heads)) for part in parts], axis=0)
    skips = jnp.concatenate([skip_ref[:, part] for part in parts], axis=0)
    small = jnp.concatenate([step, jnp.exp(-step * rates), skips], axis=0)
    wide = jnp.dot(small, spread, precision=highest, preferred_element_type=F32)

    def unfold(rows):
        return jnp.concatenate([rows[q * 4 : (q + 1) * 4] for q in range(4)], axis=1)

    sums = [jnp.zeros((1, 1), F32)] * 4
    for t in range(TP):
        x = unfold(inputs[t, DEC_X : DEC_X + 16, :].astype(F32))
        z = unfold(inputs[t, DEC_X + 16 : DEC_X + 32, :].astype(F32))
        gate = z / (1.0 + jnp.exp(-z))
        chunks = [t * CHUNKS + i for i in range(CHUNKS)]
        state = jnp.concatenate(
            [fin[k // PARTS, k % PARTS * NS : (k % PARTS + 1) * NS, :].astype(F32) for k in chunks], axis=1
        )
        skip = wide[8 * TP + t : 8 * TP + t + 1]
        for k in range(4):
            wide_step = wide[4 * t + k : 4 * t + k + 1]
            fade = wide[4 * TP + 4 * t + k : 4 * TP + 4 * t + k + 1]
            state = fade * state + b_cols[k] * (wide_step * x[k : k + 1])
            read = jnp.sum(c_cols[k] * state, axis=0, keepdims=True) + skip * x[k : k + 1]
            v = read * gate[k : k + 1]
            res[t, NS + k : NS + k + 1, :] = v
            sums[k] = sums[k] + jnp.sum(v * v, axis=1, keepdims=True)
        res[t, :NS, :] = state
    factor = jnp.concatenate([lax.rsqrt(sums[k] / WIDTH + 1e-05) for k in range(4)], axis=0)
    for t in range(TP):
        res[t, NS : NS + 4, :] = res[t, NS : NS + 4, :] * factor
        res[t, NS + 4 :, :] = jnp.zeros((4, WC), F32)
    for z in range(ROW):
        own[z] = res[2 * z + core]
        other[z] = res[2 * z + 1 - core]


def decode(inputs, maps, rate, skip, finals):
    return pl.pallas_call(
        decode_kernel,
        out_shape=[jax.ShapeDtypeStruct((ROW, NS + 8, WC), F32)] * 2,
        in_specs=[VM] * (4 + ROW),
        out_specs=[VM] * 2,
        scratch_shapes=[
            pltpu.VMEM((ROW, FINAL_ROWS, LANE), BF16),
            pltpu.VMEM((TP, NS + 8, WC), F32),
        ],
        cost_estimate=cost(4),
        compiler_params=params(),
        name="decode",
    )(inputs, maps, rate, skip, *finals)


def side_kernel(group_ref, own, other, *outs):
    me = lax.axis_index("tp")
    z, core = lax.div(me, 2), lax.rem(me, 2)
    mine = lax.rem(lax.div(my_prompt(group_ref), 2), 2) == core
    for o in range(ROW):
        at = lax.rem(z + o, ROW)
        outs[o][...] = jnp.where(mine, own[at], other[at])


def choose_side(group_of, own, other):
    return pl.pallas_call(
        side_kernel,
        out_shape=[jax.ShapeDtypeStruct((NS + 8, WC), F32)] * ROW,
        in_specs=[SM, VM, VM],
        out_specs=[VM] * ROW,
        cost_estimate=cost(1),
        compiler_params=params(),
        name="choose_side",
    )(group_of, own, other)


def along_z(arrays):
    moves = [[(i, (i + 2 * o) % TP) for i in range(TP)] for o in range(ROW)]
    return [arrays[0]] + [lax.ppermute(arrays[o], "tp", moves[o]) for o in range(1, ROW)]


def along_y(arrays):
    moves = [[(x * ROW + y, x * ROW + (y + o) % ROW) for x in range(ROW) for y in range(ROW)] for o in range(ROW)]
    return [arrays[0]] + [lax.ppermute(arrays[o], "seq", moves[o]) for o in range(1, ROW)]


def shards(
    x_in, dt_raw, bc_in, decay_rate, skip_gain, kv_pre, lengths, group_of, slot_of,
    dec_x, dec_dt, dec_bc, dec_z, norm_gain, dec_q, dec_kv,
):
    rate = decay_rate.reshape(1, HEADS)
    skip = skip_gain.reshape(1, HEADS)
    gain = norm_gain.reshape(1, -1)
    maps = jnp.swapaxes(bc_in, 1, 2)
    table = jnp.concatenate([group_of, lengths, slot_of.reshape(-1)])

    *local, sent = local_states(lengths, x_in, dt_raw, maps, rate, kv_pre, dec_x, dec_z, dec_dt)
    pages = lax.all_to_all(sent, "tp", split_axis=0, concat_axis=0, tiled=True)
    blocks = along_y(local)
    own = row_totals(blocks)
    near = lax.ppermute(own, "seq", [(i, i ^ ROW) for i in range(SEQ)])
    across = [(x * ROW + y, (ROW - 1 - x) * ROW + y) for x in range(ROW) for y in range(ROW)]
    far = lax.ppermute(pair_totals(own, near), "seq", across)
    pages, unused = lax.optimization_barrier((pages, far))
    entering = along_y(enter_states(group_of, own, near, far, blocks))
    ordered, entering = lax.optimization_barrier((order_pages(group_of, pages), entering))
    recv = lax.all_to_all(ordered, "seq", split_axis=0, concat_axis=0, tiled=True)
    own, other = decode(pages, dec_bc, rate, skip, entering)
    other = lax.ppermute(other, "tp", [(i, i ^ 1) for i in range(TP)])
    results = along_z(choose_side(group_of, own, other))
    y_pre = block_outputs(lengths, x_in, dt_raw, maps, rate, skip, entering)
    kv_pool, dec_attn, dec_state, dec_mamba = attend(
        table, recv, dec_q, dec_kv, gain, results
    )
    return (y_pre, kv_pool, dec_mamba, dec_state, dec_attn)


def solution(mesh):
    return jax.shard_map(
        shards,
        mesh=mesh,
        in_specs=(
            P("tp", "seq", None),
            P("tp", "seq", None),
            P("tp", "seq", None),
            P(),
            P(),
            P("tp", "seq", None),
            P(),
            P(),
            P(),
            P("seq", None, "tp"),
            P("seq", None, "tp"),
            P("seq", None, None),
            P("seq", None, "tp"),
            P("tp"),
            P("seq", None, "tp"),
            P("seq", None, "tp"),
        ),
        out_specs=(
            P("tp", "seq", None),
            P("seq", None, "tp"),
            P("seq", None, "tp"),
            P("seq", None, "tp"),
            P("seq", None, "tp"),
        ),
        check_vma=False,
    )
```

```python
import jax
import jax.numpy as jnp
from jax import lax
from jax.experimental import pallas as pl
from jax.experimental.pallas import tpu as pltpu
from jax.sharding import PartitionSpec as P

HD = 128
BLK = 256
HP = 64
NS = 16
HEADS = 128
WIDTH = 8192
SEQ = 16
TP = 8
WC = 1024
LANE = 128
CHUNKS = WC // LANE
STEPS = WIDTH // WC
ROW = 4
PARTS = WIDTH // (ROW * LANE)
STATE_ROWS = 2 * PARTS * NS
FINAL_ROWS = PARTS * NS
DEC_X = 2 * BLK
PAGE_ROWS = 2 * BLK + 48
F32 = jnp.float32
BF16 = jnp.bfloat16
MIB = 1024 * 1024
KV_PARTS = 2
highest = lax.Precision.HIGHEST
ANY = pl.BlockSpec(memory_space=pl.ANY)
VM = pl.BlockSpec(memory_space=pltpu.VMEM)
SM = pl.BlockSpec(memory_space=pltpu.SMEM)


def params(mib=44):
    return pltpu.CompilerParams(vmem_limit_bytes=mib * MIB)


def cost(us):
    return pl.CostEstimate(flops=0, bytes_accessed=int(us * 3.0e6), transcendentals=0)


def softplus(v):
    return jnp.maximum(v, 0.0) + jnp.log1p(jnp.exp(-jnp.abs(v)))


def halves(v):
    high = v.astype(BF16)
    return high, (v - high.astype(F32)).astype(BF16)


def fetch(pairs, sem, first=0):
    copies = [pltpu.make_async_copy(src, dst, sem.at[first + n]) for n, (src, dst) in enumerate(pairs)]
    for c in copies:
        c.start()
    return copies


def split_start(kv, x_hbm, z_hbm, dt_hbm, out, buf, x_buf, z_buf, dt_buf, rows, sem, out_sem):
    small = fetch([(x_hbm.at[0], x_buf), (z_hbm.at[0], z_buf), (dt_hbm.at[0], dt_buf)], sem, 2 * TP)
    parts = [(i, pl.ds(q * BLK // KV_PARTS, BLK // KV_PARTS)) for i in range(2) for q in range(KV_PARTS)]
    arrive = fetch([(kv.at[part], buf.at[part]) for part in parts], sem)

    def fold(part):
        part = part.astype(F32)
        return jnp.concatenate([part[:, q * 256 : (q + 1) * 256] for q in range(4)], axis=0)

    def finish():
        for c in small:
            c.wait()
        rows[:16, :] = fold(x_buf[...]).astype(BF16)
        rows[16:32, :] = fold(z_buf[...]).astype(BF16)
        steps = dt_buf[...].astype(F32)
        steps = jnp.concatenate([steps, jnp.zeros((steps.shape[0], 256 - steps.shape[1]), F32)], axis=1)
        steps = jnp.concatenate([steps, jnp.zeros((12, 256), F32)], axis=0)
        rows[32:, :] = steps.astype(BF16)
        leave = fetch([(rows, out.at[h, pl.ds(DEC_X, 48), :]) for h in range(TP)], out_sem)
        for i in range(2):
            for c in arrive[KV_PARTS * i : KV_PARTS * (i + 1)]:
                c.wait()
            heads = [(h, pl.ds(h * 2 * HD, 2 * HD)) for h in range(TP)]
            leave += fetch(
                [(buf.at[i, :, cols], out.at[h, pl.ds(i * BLK, BLK), :]) for h, cols in heads], out_sem, TP * (1 + i)
            )
        return leave

    return finish


def spread_matrix(ebig):
    rows = lax.broadcasted_iota(jnp.int32, ebig.shape, 0)
    cols = lax.broadcasted_iota(jnp.int32, ebig.shape, 1)
    ebig[...] = jnp.where((rows & (HEADS - 1)) == (cols >> 6), 1.0, 0.0).astype(BF16)


def spread_rows(ebig, j):
    start = pl.multiple_of(HEADS - (WC // HP) * j, 16)
    return ebig[pl.ds(start, 2 * HEADS), :]


def decays(len_ref, dt_ref, rate_ref, p):
    prompt = lax.axis_index("tp") * 2 + p
    live = jnp.where(len_ref[prompt] > lax.axis_index("seq") * BLK, 1.0, 0.0).astype(F32)
    step = softplus(dt_ref[p].astype(F32)) * live
    rows = lax.broadcasted_iota(jnp.int32, (BLK, BLK), 0)
    cols = lax.broadcasted_iota(jnp.int32, (BLK, BLK), 1)
    tri = jnp.where(rows >= cols, 1.0, 0.0).astype(F32)
    cum = jnp.dot(tri, -step * rate_ref[...], precision=highest, preferred_element_type=F32)
    mid = 0.5 * cum[BLK - 1 :, :]
    return live, step, cum - mid, mid


def block_copies(hbm, buf, sem, out=False):
    copies = []
    for p in range(2):
        for j in range(STEPS):
            cols = pl.ds(j * WC, WC)
            ends = (hbm.at[p, :, cols], buf.at[p, :, cols])
            copies.append(pltpu.make_async_copy(*(ends[::-1] if out else ends), sem.at[p * STEPS + j]))
    return copies


def block_copy(hbm, buf, sem, p, j, out=False):
    cols = pl.ds(pl.multiple_of(j * WC, WC), WC)
    ends = (hbm.at[p, :, cols], buf.at[p, :, cols])
    return pltpu.make_async_copy(*(ends[::-1] if out else ends), sem.at[p * STEPS + j])


def local_kernel(len_ref, x_hbm, dt_hbm, bc_hbm, rate_hbm, kv, dx_hbm, dz_hbm, ddt_hbm, *refs):
    outs, split, (stage, ft, bt, x_buf, dt_ref, bc_ref, rate_ref, sem), rest = (
        refs[:ROW],
        refs[ROW],
        refs[ROW + 1 : ROW + 9],
        refs[ROW + 9 :],
    )
    small = fetch([(dt_hbm, dt_ref), (bc_hbm, bc_ref), (rate_hbm, rate_ref)], sem, 2 * STEPS)
    x_copies = block_copies(x_hbm, x_buf, sem)
    for c in x_copies[:STEPS]:
        c.start()
    finish = split_start(kv, dx_hbm, dz_hbm, ddt_hbm, split, *rest)
    for c in x_copies[STEPS:]:
        c.start()
    for c in small:
        c.wait()
    lane = lax.broadcasted_iota(jnp.int32, (NS, LANE), 1)
    row = lax.broadcasted_iota(jnp.int32, (NS, HEADS), 0)
    heads = WC // HP
    dec = jnp.zeros((NS, HEADS), F32)
    for p in range(2):
        live, step, rel, mid = decays(len_ref, dt_ref, rate_ref, p)
        ft[p] = jnp.transpose(jnp.exp(-rel) * step)
        bt[p] = bc_ref[p, :NS, :].astype(F32)
        high, low = halves(jnp.exp(mid))
        dec = jnp.where(row == p, high.astype(F32), jnp.where(row == 2 + p, low.astype(F32), dec))
    for s in range(ROW):
        stage[s, STATE_ROWS:, :] = dec.astype(BF16)
    for p in range(2):
        if p == 1:
            leave = finish()

        def body(j, carry):
            quarter, part = lax.div(j, 2), lax.rem(j, 2)
            block_copy(x_hbm, x_buf, sem, p, j).wait()
            fj = ft[p, pl.ds(pl.multiple_of(j * heads, heads), heads), :]
            for u in range(WC // 256):
                left = jnp.concatenate([bt[p] * fj[u * 4 + h : u * 4 + h + 1, :] for h in range(4)], axis=0)
                cols = pl.ds(pl.multiple_of(j * WC + u * 256, 256), 256)
                prod = jnp.dot(left.astype(BF16), x_buf[p, :, cols], preferred_element_type=F32)
                for v in range(2):
                    cols = slice(v * LANE, (v + 1) * LANE)
                    first = prod[2 * v * NS : (2 * v + 1) * NS, cols]
                    second = prod[(2 * v + 1) * NS : (2 * v + 2) * NS, cols]
                    local = jnp.where(lane < HP, first, second).astype(BF16)
                    at = ((p * 2 + part) * CHUNKS + u * 2 + v) * NS
                    stage[quarter, pl.ds(pl.multiple_of(at, NS), NS), :] = local
            return carry

        lax.fori_loop(0, STEPS, body, 0)
    y = lax.rem(lax.axis_index("seq"), ROW)
    leave += fetch([(stage.at[lax.rem(y + o, ROW)], outs[o]) for o in range(ROW)], sem, 2 * STEPS)
    for c in leave:
        c.wait()


def local_states(lengths, x_in, dt_raw, bc_in, rate, kv_pre, dec_x, dec_z, dec_dt):
    return pl.pallas_call(
        local_kernel,
        out_shape=[jax.ShapeDtypeStruct((STATE_ROWS + NS, LANE), BF16)] * ROW
        + [jax.ShapeDtypeStruct((TP, PAGE_ROWS, 2 * HD), BF16)],
        in_specs=[SM] + [ANY] * 8,
        out_specs=[ANY] * (ROW + 1),
        scratch_shapes=[
            pltpu.VMEM((ROW, STATE_ROWS + NS, LANE), BF16),
            pltpu.VMEM((2, HEADS, BLK), F32),
            pltpu.VMEM((2, NS, BLK), F32),
            pltpu.VMEM((2, BLK, WIDTH), BF16),
            pltpu.VMEM((2, BLK, HEADS), BF16),
            pltpu.VMEM((2, 2 * NS, BLK), BF16),
            pltpu.VMEM((1, HEADS), F32),
            pltpu.SemaphoreType.DMA((2 * STEPS + ROW,)),
            pltpu.VMEM((2, BLK, TP * 2 * HD), BF16),
            pltpu.VMEM((4, WC), BF16),
            pltpu.VMEM((4, WC), BF16),
            pltpu.VMEM((4, WC // HP), BF16),
            pltpu.VMEM((48, 2 * HD), BF16),
            pltpu.SemaphoreType.DMA((2 * TP + 3,)),
            pltpu.SemaphoreType.DMA((3 * TP,)),
        ],
        cost_estimate=cost(6),
        compiler_params=params(60),
        name="local_states",
    )(lengths, x_in, dt_raw, bc_in, rate, kv_pre, dec_x, dec_z, dec_dt)


def place(arrays, scratch, me):
    for o in range(ROW):
        scratch[lax.rem(me + ROW - o, ROW)] = arrays[o][...]


def spread_decays(blocks, y):
    rows = lax.broadcasted_iota(jnp.int32, (HEADS, PARTS * LANE), 0)
    cols = lax.broadcasted_iota(jnp.int32, (HEADS, PARTS * LANE), 1)
    pick = jnp.where(rows == y * (PARTS * 2) + (cols >> 6), 1.0, 0.0).astype(BF16)
    return jnp.dot(jnp.concatenate(blocks, axis=0), pick, preferred_element_type=F32)


def decay_of(wide, block, p, c):
    cols = slice(c * LANE, (c + 1) * LANE)
    return wide[block * NS + p : block * NS + p + 1, cols] + wide[block * NS + 2 + p : block * NS + 3 + p, cols]


def groups():
    return [(p, c, (p * PARTS + c) * NS) for p in range(2) for c in range(PARTS)]


def row_kernel(*refs):
    ins, out, scr = refs[:ROW], refs[ROW], refs[ROW + 1]
    y = lax.rem(lax.axis_index("seq"), ROW)
    place(ins, scr, y)
    wide = spread_decays([scr[b, STATE_ROWS:, :] for b in range(ROW)], y)
    for p, c, at in groups():
        state = jnp.zeros((NS, LANE), F32)
        for b in range(ROW):
            half = decay_of(wide, b, p, c)
            state = half * (half * state + scr[b, at : at + NS, :].astype(F32))
        out[at : at + NS, :] = state.astype(BF16)
    once = [scr[b, STATE_ROWS:, :].astype(F32) for b in range(ROW)]
    out[STATE_ROWS:, :] = compact_decays(once + once)


def row_totals(blocks):
    return pl.pallas_call(
        row_kernel,
        out_shape=jax.ShapeDtypeStruct((STATE_ROWS + NS, LANE), BF16),
        in_specs=[VM] * ROW,
        out_specs=VM,
        scratch_shapes=[pltpu.VMEM((ROW, STATE_ROWS + NS, LANE), BF16)],
        cost_estimate=cost(1),
        compiler_params=params(),
        name="row_totals",
    )(*blocks)


def compact_decays(parts):
    row = lax.broadcasted_iota(jnp.int32, (NS, LANE), 0)
    dec = jnp.zeros((NS, LANE), F32)
    for p in range(2):
        product = jnp.ones((1, LANE), F32)
        for part in parts:
            product = product * (part[p : p + 1, :] + part[2 + p : 3 + p, :])
        high, low = halves(product)
        dec = jnp.where(row == p, high.astype(F32), jnp.where(row == 2 + p, low.astype(F32), dec))
    return dec.astype(BF16)


def place_pair(own, near, scratch, x):
    scratch[lax.rem(x, 2)] = own[...]
    scratch[1 - lax.rem(x, 2)] = near[...]


def pair_kernel(own, near, out, rows):
    me = lax.axis_index("seq")
    x, y = lax.div(me, ROW), lax.rem(me, ROW)
    place_pair(own, near, rows, x)
    wide = spread_decays([rows[1, STATE_ROWS:, :]], y)
    for p, c, at in groups():
        first, second = (rows[b, at : at + NS, :].astype(F32) for b in range(2))
        out[at : at + NS, :] = (decay_of(wide, 0, p, c) * first + second).astype(BF16)
    out[STATE_ROWS:, :] = compact_decays([rows[b, STATE_ROWS:, :].astype(F32) for b in range(2)])


def pair_totals(own, near):
    return pl.pallas_call(
        pair_kernel,
        out_shape=jax.ShapeDtypeStruct((STATE_ROWS + NS, LANE), BF16),
        in_specs=[VM] * 2,
        out_specs=VM,
        scratch_shapes=[pltpu.VMEM((2, STATE_ROWS + NS, LANE), BF16)],
        cost_estimate=cost(1),
        compiler_params=params(),
        name="pair_totals",
    )(own, near)


def enter_kernel(group_ref, own, near, far, *refs):
    blocks, outs = refs[:ROW], refs[ROW : 2 * ROW]
    scr, rows, final, stage = refs[2 * ROW :]
    me = lax.axis_index("seq")
    x, y = lax.div(me, ROW), lax.rem(me, ROW)
    place(blocks, scr, y)
    place_pair(own, near, rows, x)
    ends = [rows[0, STATE_ROWS:, :], rows[1, STATE_ROWS:, :], far[STATE_ROWS:, :]]
    wide = spread_decays([scr[b, STATE_ROWS:, :] for b in range(ROW)] + ends + ends[:1], y)
    late, odd = x >= 2, lax.rem(x, 2) == 1
    for p, c, at in groups():
        first, second = (rows[b, at : at + NS, :].astype(F32) for b in range(2))
        other = far[at : at + NS, :].astype(F32)
        before = jnp.where(late, other, 0.0)
        middle = decay_of(wide, ROW, p, c) * before + first
        after = decay_of(wide, ROW + 1, p, c) * middle + second
        final[at : at + NS, :] = jnp.where(late, after, decay_of(wide, ROW + 2, p, c) * after + other)
        state = jnp.where(odd, middle, before)
        for b in range(ROW):
            half = decay_of(wide, b, p, c)
            entering = half * state
            stage[b, at : at + NS, :] = entering.astype(BF16)
            state = half * (entering + scr[b, at : at + NS, :].astype(F32))
    second = group_ref[lax.axis_index("tp") * 2 + 1]
    for b in range(ROW):
        at = jnp.where(second == x * ROW + b, FINAL_ROWS, 0)
        chosen = final[pl.ds(pl.multiple_of(at, FINAL_ROWS), FINAL_ROWS), :]
        stage[b, STATE_ROWS:, :] = chosen.astype(BF16)
    for o in range(ROW):
        outs[o][...] = stage[lax.rem(y + o, ROW)]


def enter_states(group_of, own, near, far, blocks):
    return pl.pallas_call(
        enter_kernel,
        out_shape=[jax.ShapeDtypeStruct((STATE_ROWS + FINAL_ROWS, LANE), BF16)] * ROW,
        in_specs=[SM] + [VM] * (3 + ROW),
        out_specs=[VM] * ROW,
        scratch_shapes=[
            pltpu.VMEM((ROW, STATE_ROWS + NS, LANE), BF16),
            pltpu.VMEM((2, STATE_ROWS + NS, LANE), BF16),
            pltpu.VMEM((STATE_ROWS, LANE), F32),
            pltpu.VMEM((ROW, STATE_ROWS + FINAL_ROWS, LANE), BF16),
        ],
        cost_estimate=cost(2),
        compiler_params=params(),
        name="enter_states",
    )(group_of, own, near, far, *blocks)


def order_kernel(group_ref, pages, out):
    for r in range(SEQ):
        at = r % 2 * BLK
        out[group_ref[r]] = pages[r // 2, at : at + BLK, :]


def order_pages(group_of, pages):
    return pl.pallas_call(
        order_kernel,
        out_shape=jax.ShapeDtypeStruct((SEQ, BLK, 2 * HD), BF16),
        in_specs=[SM, VM],
        out_specs=VM,
        cost_estimate=cost(2),
        compiler_params=params(),
        name="order_pages",
    )(group_of, pages)


def spread(values, j, i):
    lanes = lax.broadcasted_iota(jnp.int32, values.shape, 1)
    return jnp.take_along_axis(values, j * (WC // HP) + 2 * i + (lanes >> 6), axis=1)


GATHERED = 8


def output_kernel(len_ref, x_hbm, dt_hbm, bc_hbm, rate_hbm, skip_hbm, *refs):
    enters, y_hbm, (after, ebig, both, mix, enter, x_buf, y_buf, dt_ref, bc_ref, rate_ref, skip_ref, c_rows, sem, out_sem) = (
        refs[:ROW],
        refs[ROW],
        refs[ROW + 1 :],
    )
    y = lax.rem(lax.axis_index("seq"), ROW)
    pairs = [(dt_hbm, dt_ref), (bc_hbm, bc_ref), (rate_hbm, rate_ref), (skip_hbm, skip_ref)]
    pairs += [(enters[o].at[pl.ds(0, STATE_ROWS), :], enter.at[lax.rem(y + ROW - o, ROW)]) for o in range(ROW)]
    small = fetch(pairs, sem, 2 * STEPS)
    for c in block_copies(x_hbm, x_buf, sem):
        c.start()
    spread_matrix(ebig)
    for c in small:
        c.wait()
    rows = lax.broadcasted_iota(jnp.int32, (BLK, BLK), 0)
    cols = lax.broadcasted_iota(jnp.int32, (BLK, BLK), 1)
    for p in range(2):
        live, step, rel, mid = decays(len_ref, dt_ref, rate_ref, p)
        after[p] = jnp.exp(rel) * live
        factors = [jnp.exp(-rel) * step, jnp.broadcast_to(skip_ref[...] * live, (NS, HEADS)), jnp.exp(rel) * live]
        for at, v in zip((0, BLK, BLK + NS), factors):
            high, low = halves(v)
            both[p, at : at + v.shape[0], :HEADS] = high
            both[p, at : at + v.shape[0], HEADS:] = low
        maps = jnp.transpose(bc_ref[p].astype(F32)).astype(BF16)
        c_rows[p] = maps[:, NS:]
        scores = jnp.dot(c_rows[p], bc_ref[p, :NS, :], preferred_element_type=F32)
        mix[p] = jnp.where(rows >= cols, scores, 0.0).astype(BF16)
    for p in range(2):

        def body(j, carry):
            block_copy(x_hbm, x_buf, sem, p, j).wait()
            at = pl.ds(pl.multiple_of(j * WC, WC), WC)
            ej = spread_rows(ebig, j)
            x = x_buf[p, :, at].astype(F32)
            factor = jnp.dot(both[p, : BLK + NS, :], ej, preferred_element_type=F32)
            xp = (x * factor[:BLK]).astype(BF16)
            first = (p * 2 + lax.rem(j, 2)) * CHUNKS * NS
            entering = enter[lax.div(j, 2), pl.ds(pl.multiple_of(first, CHUNKS * NS), CHUNKS * NS), :]
            entering = jnp.concatenate([entering[i * NS : (i + 1) * NS] for i in range(CHUNKS)], axis=1)
            total = jnp.dot(mix[p], xp, preferred_element_type=F32) + jnp.dot(
                c_rows[p], entering, preferred_element_type=F32
            )
            scales = [spread(after[p], j, i) for i in range(GATHERED)]
            if GATHERED < CHUNKS:
                scales.append(jnp.dot(both[p, BLK + NS :, :], ej[:, GATHERED * LANE :], preferred_element_type=F32))
            scale = jnp.concatenate(scales, axis=1)
            y_buf[p, :, at] = (scale * total + factor[BLK : BLK + 1] * x).astype(BF16)
            block_copy(y_hbm, y_buf, out_sem, p, j, out=True).start()
            return carry

        lax.fori_loop(0, STEPS, body, 0)
    for c in block_copies(y_hbm, y_buf, out_sem, out=True):
        c.wait()


def block_outputs(lengths, x_in, dt_raw, bc_in, rate, skip, entering):
    return pl.pallas_call(
        output_kernel,
        out_shape=jax.ShapeDtypeStruct((2, BLK, WIDTH), BF16),
        in_specs=[SM] + [ANY] * (5 + ROW),
        out_specs=ANY,
        scratch_shapes=[
            pltpu.VMEM((2, BLK, HEADS), F32),
            pltpu.VMEM((3 * HEADS, WC), BF16),
            pltpu.VMEM((2, 2 * BLK + NS, 2 * HEADS), BF16),
            pltpu.VMEM((2, BLK, BLK), BF16),
            pltpu.VMEM((ROW, STATE_ROWS, LANE), BF16),
            pltpu.VMEM((2, BLK, WIDTH), BF16),
            pltpu.VMEM((2, BLK, WIDTH), BF16),
            pltpu.VMEM((2, BLK, HEADS), BF16),
            pltpu.VMEM((2, 2 * NS, BLK), BF16),
            pltpu.VMEM((1, HEADS), F32),
            pltpu.VMEM((1, HEADS), F32),
            pltpu.VMEM((2, BLK, NS), BF16),
            pltpu.SemaphoreType.DMA((2 * STEPS + 4 + ROW,)),
            pltpu.SemaphoreType.DMA((2 * STEPS,)),
        ],
        cost_estimate=cost(12),
        compiler_params=params(54),
        name="block_outputs",
    )(lengths, x_in, dt_raw, bc_in, rate, skip, *entering)


def my_prompt(group_ref):
    mine = lax.axis_index("seq")
    prompt = jnp.int32(0)
    for r in range(SEQ):
        prompt = jnp.where(group_ref[r] == mine, r, prompt)
    return prompt


def attend_kernel(
    table, recv, q_ref, fresh_ref, gain_ref, *refs
):
    results, (pool, *outs), scratch = refs[:ROW], refs[ROW : ROW + 4], refs[ROW + 4 :]
    zeros, best, out_ref, mamba_ref, out_sem, sem = scratch
    prompt = my_prompt(table)
    length = table[SEQ + prompt]
    distance = lax.rem(lax.div(lax.axis_index("tp"), 2) + ROW - lax.div(prompt, 4), ROW)
    for o in range(ROW):

        @pl.when(distance == o)
        def _():
            best[...] = results[o][...]

    mamba_ref[0] = (best[NS : NS + 4, :] * gain_ref[...].astype(F32)).astype(BF16)
    ends = fetch([(best.at[pl.ds(0, NS), :], outs[1].at[0]), (mamba_ref, outs[2])], out_sem)
    zeros[...] = jnp.zeros(zeros.shape, BF16)

    def page_copy(s, live):
        at = pl.ds(pl.multiple_of(table[(2 + prompt) * SEQ + s] * BLK, BLK), BLK)
        source = recv.at[s] if live else zeros
        return pltpu.make_async_copy(source, pool.at[0, at, :], sem.at[s])

    for s in range(SEQ):

        @pl.when(length > s * BLK)
        def _():
            page_copy(s, True).start()

        @pl.when(length <= s * BLK)
        def _():
            page_copy(s, False).start()

    q = q_ref[0].astype(F32)
    q = jnp.concatenate([q[:, h * HD : (h + 1) * HD] for h in range(WC // HD)], axis=0).astype(BF16)
    fresh = fresh_ref[0].astype(F32)
    fresh = jnp.concatenate([fresh, jnp.zeros((12, 2 * HD), F32)], axis=0).astype(BF16)
    scale = HD**-0.5
    contract = (((1,), (1,)), ((), ()))
    rows = lax.broadcasted_iota(jnp.int32, (q.shape[0], fresh.shape[0]), 0)
    cols = lax.broadcasted_iota(jnp.int32, (q.shape[0], fresh.shape[0]), 1)
    new = lax.dot_general(q, fresh[:, :HD], contract, preferred_element_type=F32) * scale
    new = jnp.where(cols <= (rows & 3), new, -1e30)
    peak = jnp.max(new, axis=1, keepdims=True)
    old = []
    for s in range(SEQ):
        part = lax.dot_general(q, recv[s, :, :HD], contract, preferred_element_type=F32) * scale
        part = jnp.where(length > s * BLK, part, -1e30)
        old.append(part)
        peak = jnp.maximum(peak, jnp.max(part, axis=1, keepdims=True))
    prob = jnp.exp(new - peak)
    total = jnp.sum(prob, axis=1, keepdims=True)
    mixed = jnp.dot(prob.astype(BF16), fresh[:, HD:], preferred_element_type=F32)
    for s in range(SEQ):
        prob = jnp.exp(old[s] - peak)
        total = total + jnp.sum(prob, axis=1, keepdims=True)
        mixed = mixed + jnp.dot(prob.astype(BF16), recv[s, :, HD:], preferred_element_type=F32)
    result = mixed / total
    steps = out_ref.shape[1]
    for h in range(q.shape[0] // steps):
        out_ref[0, :, h * HD : (h + 1) * HD] = result[h * steps : (h + 1) * steps].astype(BF16)
    ends += fetch([(out_ref, outs[0])], out_sem, 2)
    for s in range(SEQ):
        page_copy(s, True).wait()
    for c in ends:
        c.wait()


def attend(table, recv, queries, fresh, gain, results):
    return pl.pallas_call(
        attend_kernel,
        out_shape=[
            jax.ShapeDtypeStruct((1, SEQ * BLK, 2 * HD), BF16),
            jax.ShapeDtypeStruct((1, 4, WC), BF16),
            jax.ShapeDtypeStruct((1, NS, WC), F32),
            jax.ShapeDtypeStruct((1, 4, WC), BF16),
        ],
        in_specs=[SM] + [VM] * (4 + ROW),
        out_specs=[ANY] * 4,
        scratch_shapes=[
            pltpu.VMEM((BLK, 2 * HD), BF16),
            pltpu.VMEM((NS + 8, WC), F32),
            pltpu.VMEM((1, 4, WC), BF16),
            pltpu.VMEM((1, 4, WC), BF16),
            pltpu.SemaphoreType.DMA((3,)),
            pltpu.SemaphoreType.DMA((SEQ,)),
        ],
        cost_estimate=cost(5),
        compiler_params=params(),
        name="attend",
    )(table, recv, queries, fresh, gain, *results)


def decode_kernel(inputs, maps_ref, rate_ref, skip_ref, *refs):
    finals, (own, other, fin, res) = refs[:ROW], refs[ROW:]
    core = lax.rem(lax.axis_index("tp"), 2)
    y = lax.rem(lax.axis_index("seq"), ROW)
    for o in range(ROW):
        fin[lax.rem(y + ROW - o, ROW)] = finals[o][STATE_ROWS:, :]
    maps = maps_ref[0].astype(F32)
    eye = lax.broadcasted_iota(jnp.int32, (NS, NS), 0) == lax.broadcasted_iota(jnp.int32, (NS, NS), 1)

    def column(k, at):
        return jnp.sum(jnp.where(eye, maps[k : k + 1, at : at + NS], 0.0), axis=1, keepdims=True)

    b_cols = [column(k, 0) for k in range(4)]
    c_cols = [column(k, NS) for k in range(4)]
    heads = WC // HP
    rows = lax.broadcasted_iota(jnp.int32, (heads, WC), 0)
    cols = lax.broadcasted_iota(jnp.int32, (heads, WC), 1)
    spread = jnp.where(rows == (cols >> 6), 1.0, 0.0).astype(F32)
    raw = [inputs[t, DEC_X + 32 : DEC_X + 48, :].astype(F32)[:4, :heads] for t in range(TP)]
    step = softplus(jnp.concatenate(raw, axis=0))
    parts = [slice(t * heads, (t + 1) * heads) for t in range(TP)]
    rates = jnp.concatenate([jnp.broadcast_to(rate_ref[:, part], (4, heads)) for part in parts], axis=0)
    skips = jnp.concatenate([skip_ref[:, part] for part in parts], axis=0)
    small = jnp.concatenate([step, jnp.exp(-step * rates), skips], axis=0)
    wide = jnp.dot(small, spread, precision=highest, preferred_element_type=F32)

    def unfold(rows):
        return jnp.concatenate([rows[q * 4 : (q + 1) * 4] for q in range(4)], axis=1)

    sums = [jnp.zeros((1, 1), F32)] * 4
    for t in range(TP):
        x = unfold(inputs[t, DEC_X : DEC_X + 16, :].astype(F32))
        z = unfold(inputs[t, DEC_X + 16 : DEC_X + 32, :].astype(F32))
        gate = z / (1.0 + jnp.exp(-z))
        chunks = [t * CHUNKS + i for i in range(CHUNKS)]
        state = jnp.concatenate(
            [fin[k // PARTS, k % PARTS * NS : (k % PARTS + 1) * NS, :].astype(F32) for k in chunks], axis=1
        )
        skip = wide[8 * TP + t : 8 * TP + t + 1]
        for k in range(4):
            wide_step = wide[4 * t + k : 4 * t + k + 1]
            fade = wide[4 * TP + 4 * t + k : 4 * TP + 4 * t + k + 1]
            state = fade * state + b_cols[k] * (wide_step * x[k : k + 1])
            read = jnp.sum(c_cols[k] * state, axis=0, keepdims=True) + skip * x[k : k + 1]
            v = read * gate[k : k + 1]
            res[t, NS + k : NS + k + 1, :] = v
            sums[k] = sums[k] + jnp.sum(v * v, axis=1, keepdims=True)
        res[t, :NS, :] = state
    factor = jnp.concatenate([lax.rsqrt(sums[k] / WIDTH + 1e-05) for k in range(4)], axis=0)
    for t in range(TP):
        res[t, NS : NS + 4, :] = res[t, NS : NS + 4, :] * factor
        res[t, NS + 4 :, :] = jnp.zeros((4, WC), F32)
    for z in range(ROW):
        own[z] = res[2 * z + core]
        other[z] = res[2 * z + 1 - core]


def decode(inputs, maps, rate, skip, finals):
    return pl.pallas_call(
        decode_kernel,
        out_shape=[jax.ShapeDtypeStruct((ROW, NS + 8, WC), F32)] * 2,
        in_specs=[VM] * (4 + ROW),
        out_specs=[VM] * 2,
        scratch_shapes=[
            pltpu.VMEM((ROW, FINAL_ROWS, LANE), BF16),
            pltpu.VMEM((TP, NS + 8, WC), F32),
        ],
        cost_estimate=cost(4),
        compiler_params=params(),
        name="decode",
    )(inputs, maps, rate, skip, *finals)


def side_kernel(group_ref, own, other, *outs):
    me = lax.axis_index("tp")
    z, core = lax.div(me, 2), lax.rem(me, 2)
    mine = lax.rem(lax.div(my_prompt(group_ref), 2), 2) == core
    for o in range(ROW):
        at = lax.rem(z + o, ROW)
        outs[o][...] = jnp.where(mine, own[at], other[at])


def choose_side(group_of, own, other):
    return pl.pallas_call(
        side_kernel,
        out_shape=[jax.ShapeDtypeStruct((NS + 8, WC), F32)] * ROW,
        in_specs=[SM, VM, VM],
        out_specs=[VM] * ROW,
        cost_estimate=cost(1),
        compiler_params=params(),
        name="choose_side",
    )(group_of, own, other)


def along_z(arrays):
    moves = [[(i, (i + 2 * o) % TP) for i in range(TP)] for o in range(ROW)]
    return [arrays[0]] + [lax.ppermute(arrays[o], "tp", moves[o]) for o in range(1, ROW)]


def along_y(arrays):
    moves = [[(x * ROW + y, x * ROW + (y + o) % ROW) for x in range(ROW) for y in range(ROW)] for o in range(ROW)]
    return [arrays[0]] + [lax.ppermute(arrays[o], "seq", moves[o]) for o in range(1, ROW)]


def shards(
    x_in, dt_raw, bc_in, decay_rate, skip_gain, kv_pre, lengths, group_of, slot_of,
    dec_x, dec_dt, dec_bc, dec_z, norm_gain, dec_q, dec_kv,
):
    rate = decay_rate.reshape(1, HEADS)
    skip = skip_gain.reshape(1, HEADS)
    gain = norm_gain.reshape(1, -1)
    maps = jnp.swapaxes(bc_in, 1, 2)
    table = jnp.concatenate([group_of, lengths, slot_of.reshape(-1)])

    *local, sent = local_states(lengths, x_in, dt_raw, maps, rate, kv_pre, dec_x, dec_z, dec_dt)
    pages = lax.all_to_all(sent, "tp", split_axis=0, concat_axis=0, tiled=True)
    blocks = along_y(local)
    own = row_totals(blocks)
    near = lax.ppermute(own, "seq", [(i, i ^ ROW) for i in range(SEQ)])
    across = [(x * ROW + y, (ROW - 1 - x) * ROW + y) for x in range(ROW) for y in range(ROW)]
    far = lax.ppermute(pair_totals(own, near), "seq", across)
    pages, unused = lax.optimization_barrier((pages, far))
    entering = along_y(enter_states(group_of, own, near, far, blocks))
    ordered, entering = lax.optimization_barrier((order_pages(group_of, pages), entering))
    recv = lax.all_to_all(ordered, "seq", split_axis=0, concat_axis=0, tiled=True)
    own, other = decode(pages, dec_bc, rate, skip, entering)
    other = lax.ppermute(other, "tp", [(i, i ^ 1) for i in range(TP)])
    results = along_z(choose_side(group_of, own, other))
    y_pre = block_outputs(lengths, x_in, dt_raw, maps, rate, skip, entering)
    kv_pool, dec_attn, dec_state, dec_mamba = attend(
        table, recv, dec_q, dec_kv, gain, results
    )
    return (y_pre, kv_pool, dec_mamba, dec_state, dec_attn)


def solution(mesh):
    return jax.shard_map(
        shards,
        mesh=mesh,
        in_specs=(
            P("tp", "seq", None),
            P("tp", "seq", None),
            P("tp", "seq", None),
            P(),
            P(),
            P("tp", "seq", None),
            P(),
            P(),
            P(),
            P("seq", None, "tp"),
            P("seq", None, "tp"),
            P("seq", None, None),
            P("seq", None, "tp"),
            P("tp"),
            P("seq", None, "tp"),
            P("seq", None, "tp"),
        ),
        out_specs=(
            P("tp", "seq", None),
            P("seq", None, "tp"),
            P("seq", None, "tp"),
            P("seq", None, "tp"),
            P("seq", None, "tp"),
        ),
        check_vma=False,
    )
```

```python
import jax
import jax.numpy as jnp
from jax import lax
from jax.experimental import pallas as pl
from jax.experimental.pallas import tpu as pltpu
from jax.sharding import PartitionSpec as P

HD = 128
BLK = 256
HP = 64
NS = 16
HEADS = 128
WIDTH = 8192
SEQ = 16
TP = 8
WC = 1024
LANE = 128
CHUNKS = WC // LANE
STEPS = WIDTH // WC
ROW = 4
PARTS = WIDTH // (ROW * LANE)
STATE_ROWS = 2 * PARTS * NS
FINAL_ROWS = PARTS * NS
DEC_X = 2 * BLK
PAGE_ROWS = 2 * BLK + 48
F32 = jnp.float32
BF16 = jnp.bfloat16
MIB = 1024 * 1024
KV_PARTS = 2
highest = lax.Precision.HIGHEST
ANY = pl.BlockSpec(memory_space=pl.ANY)
VM = pl.BlockSpec(memory_space=pltpu.VMEM)
SM = pl.BlockSpec(memory_space=pltpu.SMEM)


def params(mib=44):
    return pltpu.CompilerParams(vmem_limit_bytes=mib * MIB)


def cost(us):
    return pl.CostEstimate(flops=0, bytes_accessed=int(us * 3.0e6), transcendentals=0)


def softplus(v):
    return jnp.maximum(v, 0.0) + jnp.log1p(jnp.exp(-jnp.abs(v)))


def halves(v):
    high = v.astype(BF16)
    return high, (v - high.astype(F32)).astype(BF16)


def fetch(pairs, sem, first=0):
    copies = [pltpu.make_async_copy(src, dst, sem.at[first + n]) for n, (src, dst) in enumerate(pairs)]
    for c in copies:
        c.start()
    return copies


def split_start(kv, x_hbm, z_hbm, dt_hbm, out, buf, x_buf, z_buf, dt_buf, rows, sem, out_sem):
    small = fetch([(x_hbm.at[0], x_buf), (z_hbm.at[0], z_buf), (dt_hbm.at[0], dt_buf)], sem, 2 * TP)
    parts = [(i, pl.ds(q * BLK // KV_PARTS, BLK // KV_PARTS)) for i in range(2) for q in range(KV_PARTS)]
    arrive = fetch([(kv.at[part], buf.at[part]) for part in parts], sem)

    def fold(part):
        part = part.astype(F32)
        return jnp.concatenate([part[:, q * 256 : (q + 1) * 256] for q in range(4)], axis=0)

    def finish():
        for c in small:
            c.wait()
        rows[:16, :] = fold(x_buf[...]).astype(BF16)
        rows[16:32, :] = fold(z_buf[...]).astype(BF16)
        steps = dt_buf[...].astype(F32)
        steps = jnp.concatenate([steps, jnp.zeros((steps.shape[0], 256 - steps.shape[1]), F32)], axis=1)
        steps = jnp.concatenate([steps, jnp.zeros((12, 256), F32)], axis=0)
        rows[32:, :] = steps.astype(BF16)
        leave = fetch([(rows, out.at[h, pl.ds(DEC_X, 48), :]) for h in range(TP)], out_sem)
        for i in range(2):
            for c in arrive[KV_PARTS * i : KV_PARTS * (i + 1)]:
                c.wait()
            heads = [(h, pl.ds(h * 2 * HD, 2 * HD)) for h in range(TP)]
            leave += fetch(
                [(buf.at[i, :, cols], out.at[h, pl.ds(i * BLK, BLK), :]) for h, cols in heads], out_sem, TP * (1 + i)
            )
        return leave

    return finish


def spread_matrix(ebig):
    rows = lax.broadcasted_iota(jnp.int32, ebig.shape, 0)
    cols = lax.broadcasted_iota(jnp.int32, ebig.shape, 1)
    ebig[...] = jnp.where((rows & (HEADS - 1)) == (cols >> 6), 1.0, 0.0).astype(BF16)


def spread_rows(ebig, j):
    start = pl.multiple_of(HEADS - (WC // HP) * j, 16)
    return ebig[pl.ds(start, 2 * HEADS), :]


def decays(len_ref, dt_ref, rate_ref, p):
    prompt = lax.axis_index("tp") * 2 + p
    live = jnp.where(len_ref[prompt] > lax.axis_index("seq") * BLK, 1.0, 0.0).astype(F32)
    step = softplus(dt_ref[p].astype(F32)) * live
    rows = lax.broadcasted_iota(jnp.int32, (BLK, BLK), 0)
    cols = lax.broadcasted_iota(jnp.int32, (BLK, BLK), 1)
    tri = jnp.where(rows >= cols, 1.0, 0.0).astype(F32)
    cum = jnp.dot(tri, -step * rate_ref[...], precision=highest, preferred_element_type=F32)
    mid = 0.5 * cum[BLK - 1 :, :]
    return live, step, cum - mid, mid


def block_copies(hbm, buf, sem, out=False):
    copies = []
    for p in range(2):
        for j in range(STEPS):
            cols = pl.ds(j * WC, WC)
            ends = (hbm.at[p, :, cols], buf.at[p, :, cols])
            copies.append(pltpu.make_async_copy(*(ends[::-1] if out else ends), sem.at[p * STEPS + j]))
    return copies


def block_copy(hbm, buf, sem, p, j, out=False):
    cols = pl.ds(pl.multiple_of(j * WC, WC), WC)
    ends = (hbm.at[p, :, cols], buf.at[p, :, cols])
    return pltpu.make_async_copy(*(ends[::-1] if out else ends), sem.at[p * STEPS + j])


def local_kernel(len_hbm, x_hbm, dt_hbm, bc_hbm, rate_hbm, kv, dx_hbm, dz_hbm, ddt_hbm, *refs):
    outs, split, (len_ref, stage, ft, bt, x_buf, dt_ref, bc_ref, rate_ref, sem), rest = (
        refs[:ROW],
        refs[ROW],
        refs[ROW + 1 : ROW + 10],
        refs[ROW + 10 :],
    )
    small = fetch([(dt_hbm, dt_ref), (bc_hbm, bc_ref), (rate_hbm, rate_ref), (len_hbm, len_ref)], sem, 2 * STEPS)
    x_copies = block_copies(x_hbm, x_buf, sem)
    for c in x_copies[:STEPS]:
        c.start()
    finish = split_start(kv, dx_hbm, dz_hbm, ddt_hbm, split, *rest)
    for c in x_copies[STEPS:]:
        c.start()
    for c in small:
        c.wait()
    lane = lax.broadcasted_iota(jnp.int32, (NS, LANE), 1)
    row = lax.broadcasted_iota(jnp.int32, (NS, HEADS), 0)
    heads = WC // HP
    dec = jnp.zeros((NS, HEADS), F32)
    for p in range(2):
        live, step, rel, mid = decays(len_ref, dt_ref, rate_ref, p)
        ft[p] = jnp.transpose(jnp.exp(-rel) * step)
        bt[p] = bc_ref[p, :NS, :].astype(F32)
        high, low = halves(jnp.exp(mid))
        dec = jnp.where(row == p, high.astype(F32), jnp.where(row == 2 + p, low.astype(F32), dec))
    for s in range(ROW):
        stage[s, STATE_ROWS:, :] = dec.astype(BF16)
    for p in range(2):
        if p == 1:
            leave = finish()

        def body(j, carry):
            quarter, part = lax.div(j, 2), lax.rem(j, 2)
            block_copy(x_hbm, x_buf, sem, p, j).wait()
            fj = ft[p, pl.ds(pl.multiple_of(j * heads, heads), heads), :]
            for u in range(WC // 256):
                left = jnp.concatenate([bt[p] * fj[u * 4 + h : u * 4 + h + 1, :] for h in range(4)], axis=0)
                cols = pl.ds(pl.multiple_of(j * WC + u * 256, 256), 256)
                prod = jnp.dot(left.astype(BF16), x_buf[p, :, cols], preferred_element_type=F32)
                for v in range(2):
                    cols = slice(v * LANE, (v + 1) * LANE)
                    first = prod[2 * v * NS : (2 * v + 1) * NS, cols]
                    second = prod[(2 * v + 1) * NS : (2 * v + 2) * NS, cols]
                    local = jnp.where(lane < HP, first, second).astype(BF16)
                    at = ((p * 2 + part) * CHUNKS + u * 2 + v) * NS
                    stage[quarter, pl.ds(pl.multiple_of(at, NS), NS), :] = local
            return carry

        lax.fori_loop(0, STEPS, body, 0)
    y = lax.rem(lax.axis_index("seq"), ROW)
    leave += fetch([(stage.at[lax.rem(y + o, ROW)], outs[o]) for o in range(ROW)], sem, 2 * STEPS)
    for c in leave:
        c.wait()


def local_states(lengths, x_in, dt_raw, bc_in, rate, kv_pre, dec_x, dec_z, dec_dt):
    return pl.pallas_call(
        local_kernel,
        out_shape=[jax.ShapeDtypeStruct((STATE_ROWS + NS, LANE), BF16)] * ROW
        + [jax.ShapeDtypeStruct((TP, PAGE_ROWS, 2 * HD), BF16)],
        in_specs=[ANY] * 9,
        out_specs=[ANY] * (ROW + 1),
        scratch_shapes=[
            pltpu.SMEM((SEQ,), jnp.int32),
            pltpu.VMEM((ROW, STATE_ROWS + NS, LANE), BF16),
            pltpu.VMEM((2, HEADS, BLK), F32),
            pltpu.VMEM((2, NS, BLK), F32),
            pltpu.VMEM((2, BLK, WIDTH), BF16),
            pltpu.VMEM((2, BLK, HEADS), BF16),
            pltpu.VMEM((2, 2 * NS, BLK), BF16),
            pltpu.VMEM((1, HEADS), F32),
            pltpu.SemaphoreType.DMA((2 * STEPS + ROW,)),
            pltpu.VMEM((2, BLK, TP * 2 * HD), BF16),
            pltpu.VMEM((4, WC), BF16),
            pltpu.VMEM((4, WC), BF16),
            pltpu.VMEM((4, WC // HP), BF16),
            pltpu.VMEM((48, 2 * HD), BF16),
            pltpu.SemaphoreType.DMA((2 * TP + 3,)),
            pltpu.SemaphoreType.DMA((3 * TP,)),
        ],
        cost_estimate=cost(6),
        compiler_params=params(60),
        name="local_states",
    )(lengths, x_in, dt_raw, bc_in, rate, kv_pre, dec_x, dec_z, dec_dt)


def place(arrays, scratch, me):
    for o in range(ROW):
        scratch[lax.rem(me + ROW - o, ROW)] = arrays[o][...]


def spread_decays(blocks, y):
    rows = lax.broadcasted_iota(jnp.int32, (HEADS, PARTS * LANE), 0)
    cols = lax.broadcasted_iota(jnp.int32, (HEADS, PARTS * LANE), 1)
    pick = jnp.where(rows == y * (PARTS * 2) + (cols >> 6), 1.0, 0.0).astype(BF16)
    return jnp.dot(jnp.concatenate(blocks, axis=0), pick, preferred_element_type=F32)


def decay_of(wide, block, p, c):
    cols = slice(c * LANE, (c + 1) * LANE)
    return wide[block * NS + p : block * NS + p + 1, cols] + wide[block * NS + 2 + p : block * NS + 3 + p, cols]


def groups():
    return [(p, c, (p * PARTS + c) * NS) for p in range(2) for c in range(PARTS)]


def row_kernel(*refs):
    ins, out, scr = refs[:ROW], refs[ROW], refs[ROW + 1]
    y = lax.rem(lax.axis_index("seq"), ROW)
    place(ins, scr, y)
    wide = spread_decays([scr[b, STATE_ROWS:, :] for b in range(ROW)], y)
    for p, c, at in groups():
        state = jnp.zeros((NS, LANE), F32)
        for b in range(ROW):
            half = decay_of(wide, b, p, c)
            state = half * (half * state + scr[b, at : at + NS, :].astype(F32))
        out[at : at + NS, :] = state.astype(BF16)
    once = [scr[b, STATE_ROWS:, :].astype(F32) for b in range(ROW)]
    out[STATE_ROWS:, :] = compact_decays(once + once)


def row_totals(blocks):
    return pl.pallas_call(
        row_kernel,
        out_shape=jax.ShapeDtypeStruct((STATE_ROWS + NS, LANE), BF16),
        in_specs=[VM] * ROW,
        out_specs=VM,
        scratch_shapes=[pltpu.VMEM((ROW, STATE_ROWS + NS, LANE), BF16)],
        cost_estimate=cost(1),
        compiler_params=params(),
        name="row_totals",
    )(*blocks)


def compact_decays(parts):
    row = lax.broadcasted_iota(jnp.int32, (NS, LANE), 0)
    dec = jnp.zeros((NS, LANE), F32)
    for p in range(2):
        product = jnp.ones((1, LANE), F32)
        for part in parts:
            product = product * (part[p : p + 1, :] + part[2 + p : 3 + p, :])
        high, low = halves(product)
        dec = jnp.where(row == p, high.astype(F32), jnp.where(row == 2 + p, low.astype(F32), dec))
    return dec.astype(BF16)


def place_pair(own, near, scratch, x):
    scratch[lax.rem(x, 2)] = own[...]
    scratch[1 - lax.rem(x, 2)] = near[...]


def pair_kernel(own, near, out, rows):
    me = lax.axis_index("seq")
    x, y = lax.div(me, ROW), lax.rem(me, ROW)
    place_pair(own, near, rows, x)
    wide = spread_decays([rows[1, STATE_ROWS:, :]], y)
    for p, c, at in groups():
        first, second = (rows[b, at : at + NS, :].astype(F32) for b in range(2))
        out[at : at + NS, :] = (decay_of(wide, 0, p, c) * first + second).astype(BF16)
    out[STATE_ROWS:, :] = compact_decays([rows[b, STATE_ROWS:, :].astype(F32) for b in range(2)])


def pair_totals(own, near):
    return pl.pallas_call(
        pair_kernel,
        out_shape=jax.ShapeDtypeStruct((STATE_ROWS + NS, LANE), BF16),
        in_specs=[VM] * 2,
        out_specs=VM,
        scratch_shapes=[pltpu.VMEM((2, STATE_ROWS + NS, LANE), BF16)],
        cost_estimate=cost(1),
        compiler_params=params(),
        name="pair_totals",
    )(own, near)


def enter_kernel(group_ref, own, near, far, *refs):
    blocks, outs = refs[:ROW], refs[ROW : 2 * ROW]
    scr, rows, final, stage = refs[2 * ROW :]
    me = lax.axis_index("seq")
    x, y = lax.div(me, ROW), lax.rem(me, ROW)
    place(blocks, scr, y)
    place_pair(own, near, rows, x)
    ends = [rows[0, STATE_ROWS:, :], rows[1, STATE_ROWS:, :], far[STATE_ROWS:, :]]
    wide = spread_decays([scr[b, STATE_ROWS:, :] for b in range(ROW)] + ends + ends[:1], y)
    late, odd = x >= 2, lax.rem(x, 2) == 1
    for p, c, at in groups():
        first, second = (rows[b, at : at + NS, :].astype(F32) for b in range(2))
        other = far[at : at + NS, :].astype(F32)
        before = jnp.where(late, other, 0.0)
        middle = decay_of(wide, ROW, p, c) * before + first
        after = decay_of(wide, ROW + 1, p, c) * middle + second
        final[at : at + NS, :] = jnp.where(late, after, decay_of(wide, ROW + 2, p, c) * after + other)
        state = jnp.where(odd, middle, before)
        for b in range(ROW):
            half = decay_of(wide, b, p, c)
            entering = half * state
            stage[b, at : at + NS, :] = entering.astype(BF16)
            state = half * (entering + scr[b, at : at + NS, :].astype(F32))
    second = group_ref[lax.axis_index("tp") * 2 + 1]
    for b in range(ROW):
        at = jnp.where(second == x * ROW + b, FINAL_ROWS, 0)
        chosen = final[pl.ds(pl.multiple_of(at, FINAL_ROWS), FINAL_ROWS), :]
        stage[b, STATE_ROWS:, :] = chosen.astype(BF16)
    for o in range(ROW):
        outs[o][...] = stage[lax.rem(y + o, ROW)]


def enter_states(group_of, own, near, far, blocks):
    return pl.pallas_call(
        enter_kernel,
        out_shape=[jax.ShapeDtypeStruct((STATE_ROWS + FINAL_ROWS, LANE), BF16)] * ROW,
        in_specs=[SM] + [VM] * (3 + ROW),
        out_specs=[VM] * ROW,
        scratch_shapes=[
            pltpu.VMEM((ROW, STATE_ROWS + NS, LANE), BF16),
            pltpu.VMEM((2, STATE_ROWS + NS, LANE), BF16),
            pltpu.VMEM((STATE_ROWS, LANE), F32),
            pltpu.VMEM((ROW, STATE_ROWS + FINAL_ROWS, LANE), BF16),
        ],
        cost_estimate=cost(2),
        compiler_params=params(),
        name="enter_states",
    )(group_of, own, near, far, *blocks)


def order_kernel(group_ref, pages, out):
    for r in range(SEQ):
        at = r % 2 * BLK
        out[group_ref[r]] = pages[r // 2, at : at + BLK, :]


def order_pages(group_of, pages):
    return pl.pallas_call(
        order_kernel,
        out_shape=jax.ShapeDtypeStruct((SEQ, BLK, 2 * HD), BF16),
        in_specs=[SM, VM],
        out_specs=VM,
        cost_estimate=cost(2),
        compiler_params=params(),
        name="order_pages",
    )(group_of, pages)


def spread(values, j, i):
    lanes = lax.broadcasted_iota(jnp.int32, values.shape, 1)
    return jnp.take_along_axis(values, j * (WC // HP) + 2 * i + (lanes >> 6), axis=1)


GATHERED = 8


def output_kernel(len_ref, x_hbm, dt_hbm, bc_hbm, rate_hbm, skip_hbm, *refs):
    enters, y_hbm, (after, ebig, both, mix, enter, x_buf, y_buf, dt_ref, bc_ref, rate_ref, skip_ref, c_rows, sem, out_sem) = (
        refs[:ROW],
        refs[ROW],
        refs[ROW + 1 :],
    )
    y = lax.rem(lax.axis_index("seq"), ROW)
    pairs = [(dt_hbm, dt_ref), (bc_hbm, bc_ref), (rate_hbm, rate_ref), (skip_hbm, skip_ref)]
    pairs += [(enters[o].at[pl.ds(0, STATE_ROWS), :], enter.at[lax.rem(y + ROW - o, ROW)]) for o in range(ROW)]
    small = fetch(pairs, sem, 2 * STEPS)
    for c in block_copies(x_hbm, x_buf, sem):
        c.start()
    spread_matrix(ebig)
    for c in small:
        c.wait()
    rows = lax.broadcasted_iota(jnp.int32, (BLK, BLK), 0)
    cols = lax.broadcasted_iota(jnp.int32, (BLK, BLK), 1)
    for p in range(2):
        live, step, rel, mid = decays(len_ref, dt_ref, rate_ref, p)
        after[p] = jnp.exp(rel) * live
        factors = [jnp.exp(-rel) * step, jnp.broadcast_to(skip_ref[...] * live, (NS, HEADS)), jnp.exp(rel) * live]
        for at, v in zip((0, BLK, BLK + NS), factors):
            high, low = halves(v)
            both[p, at : at + v.shape[0], :HEADS] = high
            both[p, at : at + v.shape[0], HEADS:] = low
        maps = jnp.transpose(bc_ref[p].astype(F32)).astype(BF16)
        c_rows[p] = maps[:, NS:]
        scores = jnp.dot(c_rows[p], bc_ref[p, :NS, :], preferred_element_type=F32)
        mix[p] = jnp.where(rows >= cols, scores, 0.0).astype(BF16)
    for p in range(2):

        def body(j, carry):
            block_copy(x_hbm, x_buf, sem, p, j).wait()
            at = pl.ds(pl.multiple_of(j * WC, WC), WC)
            ej = spread_rows(ebig, j)
            x = x_buf[p, :, at].astype(F32)
            factor = jnp.dot(both[p, : BLK + NS, :], ej, preferred_element_type=F32)
            xp = (x * factor[:BLK]).astype(BF16)
            first = (p * 2 + lax.rem(j, 2)) * CHUNKS * NS
            entering = enter[lax.div(j, 2), pl.ds(pl.multiple_of(first, CHUNKS * NS), CHUNKS * NS), :]
            entering = jnp.concatenate([entering[i * NS : (i + 1) * NS] for i in range(CHUNKS)], axis=1)
            total = jnp.dot(mix[p], xp, preferred_element_type=F32) + jnp.dot(
                c_rows[p], entering, preferred_element_type=F32
            )
            scales = [spread(after[p], j, i) for i in range(GATHERED)]
            if GATHERED < CHUNKS:
                scales.append(jnp.dot(both[p, BLK + NS :, :], ej[:, GATHERED * LANE :], preferred_element_type=F32))
            scale = jnp.concatenate(scales, axis=1)
            y_buf[p, :, at] = (scale * total + factor[BLK : BLK + 1] * x).astype(BF16)
            block_copy(y_hbm, y_buf, out_sem, p, j, out=True).start()
            return carry

        lax.fori_loop(0, STEPS, body, 0)
    for c in block_copies(y_hbm, y_buf, out_sem, out=True):
        c.wait()


def block_outputs(lengths, x_in, dt_raw, bc_in, rate, skip, entering):
    return pl.pallas_call(
        output_kernel,
        out_shape=jax.ShapeDtypeStruct((2, BLK, WIDTH), BF16),
        in_specs=[SM] + [ANY] * (5 + ROW),
        out_specs=ANY,
        scratch_shapes=[
            pltpu.VMEM((2, BLK, HEADS), F32),
            pltpu.VMEM((3 * HEADS, WC), BF16),
            pltpu.VMEM((2, 2 * BLK + NS, 2 * HEADS), BF16),
            pltpu.VMEM((2, BLK, BLK), BF16),
            pltpu.VMEM((ROW, STATE_ROWS, LANE), BF16),
            pltpu.VMEM((2, BLK, WIDTH), BF16),
            pltpu.VMEM((2, BLK, WIDTH), BF16),
            pltpu.VMEM((2, BLK, HEADS), BF16),
            pltpu.VMEM((2, 2 * NS, BLK), BF16),
            pltpu.VMEM((1, HEADS), F32),
            pltpu.VMEM((1, HEADS), F32),
            pltpu.VMEM((2, BLK, NS), BF16),
            pltpu.SemaphoreType.DMA((2 * STEPS + 4 + ROW,)),
            pltpu.SemaphoreType.DMA((2 * STEPS,)),
        ],
        cost_estimate=cost(12),
        compiler_params=params(54),
        name="block_outputs",
    )(lengths, x_in, dt_raw, bc_in, rate, skip, *entering)


def my_prompt(group_ref):
    mine = lax.axis_index("seq")
    prompt = jnp.int32(0)
    for r in range(SEQ):
        prompt = jnp.where(group_ref[r] == mine, r, prompt)
    return prompt


def attend_kernel(
    table, recv, q_ref, fresh_ref, gain_ref, *refs
):
    results, (pool, *outs), scratch = refs[:ROW], refs[ROW : ROW + 4], refs[ROW + 4 :]
    zeros, best, out_ref, mamba_ref, out_sem, sem = scratch
    prompt = my_prompt(table)
    length = table[SEQ + prompt]
    distance = lax.rem(lax.div(lax.axis_index("tp"), 2) + ROW - lax.div(prompt, 4), ROW)
    for o in range(ROW):

        @pl.when(distance == o)
        def _():
            best[...] = results[o][...]

    mamba_ref[0] = (best[NS : NS + 4, :] * gain_ref[...].astype(F32)).astype(BF16)
    ends = fetch([(best.at[pl.ds(0, NS), :], outs[1].at[0]), (mamba_ref, outs[2])], out_sem)
    zeros[...] = jnp.zeros(zeros.shape, BF16)

    def page_copy(s, live):
        at = pl.ds(pl.multiple_of(table[(2 + prompt) * SEQ + s] * BLK, BLK), BLK)
        source = recv.at[s] if live else zeros
        return pltpu.make_async_copy(source, pool.at[0, at, :], sem.at[s])

    for s in range(SEQ):

        @pl.when(length > s * BLK)
        def _():
            page_copy(s, True).start()

        @pl.when(length <= s * BLK)
        def _():
            page_copy(s, False).start()

    q = q_ref[0].astype(F32)
    q = jnp.concatenate([q[:, h * HD : (h + 1) * HD] for h in range(WC // HD)], axis=0).astype(BF16)
    fresh = fresh_ref[0].astype(F32)
    fresh = jnp.concatenate([fresh, jnp.zeros((12, 2 * HD), F32)], axis=0).astype(BF16)
    scale = HD**-0.5
    contract = (((1,), (1,)), ((), ()))
    rows = lax.broadcasted_iota(jnp.int32, (q.shape[0], fresh.shape[0]), 0)
    cols = lax.broadcasted_iota(jnp.int32, (q.shape[0], fresh.shape[0]), 1)
    new = lax.dot_general(q, fresh[:, :HD], contract, preferred_element_type=F32) * scale
    new = jnp.where(cols <= (rows & 3), new, -1e30)
    peak = jnp.max(new, axis=1, keepdims=True)
    old = []
    for s in range(SEQ):
        part = lax.dot_general(q, recv[s, :, :HD], contract, preferred_element_type=F32) * scale
        part = jnp.where(length > s * BLK, part, -1e30)
        old.append(part)
        peak = jnp.maximum(peak, jnp.max(part, axis=1, keepdims=True))
    prob = jnp.exp(new - peak)
    total = jnp.sum(prob, axis=1, keepdims=True)
    mixed = jnp.dot(prob.astype(BF16), fresh[:, HD:], preferred_element_type=F32)
    for s in range(SEQ):
        prob = jnp.exp(old[s] - peak)
        total = total + jnp.sum(prob, axis=1, keepdims=True)
        mixed = mixed + jnp.dot(prob.astype(BF16), recv[s, :, HD:], preferred_element_type=F32)
    result = mixed / total
    steps = out_ref.shape[1]
    for h in range(q.shape[0] // steps):
        out_ref[0, :, h * HD : (h + 1) * HD] = result[h * steps : (h + 1) * steps].astype(BF16)
    ends += fetch([(out_ref, outs[0])], out_sem, 2)
    for s in range(SEQ):
        page_copy(s, True).wait()
    for c in ends:
        c.wait()


def attend(table, recv, queries, fresh, gain, results):
    return pl.pallas_call(
        attend_kernel,
        out_shape=[
            jax.ShapeDtypeStruct((1, SEQ * BLK, 2 * HD), BF16),
            jax.ShapeDtypeStruct((1, 4, WC), BF16),
            jax.ShapeDtypeStruct((1, NS, WC), F32),
            jax.ShapeDtypeStruct((1, 4, WC), BF16),
        ],
        in_specs=[SM] + [VM] * (4 + ROW),
        out_specs=[ANY] * 4,
        scratch_shapes=[
            pltpu.VMEM((BLK, 2 * HD), BF16),
            pltpu.VMEM((NS + 8, WC), F32),
            pltpu.VMEM((1, 4, WC), BF16),
            pltpu.VMEM((1, 4, WC), BF16),
            pltpu.SemaphoreType.DMA((3,)),
            pltpu.SemaphoreType.DMA((SEQ,)),
        ],
        cost_estimate=cost(5),
        compiler_params=params(54),
        name="attend",
    )(table, recv, queries, fresh, gain, *results)


def decode_kernel(inputs, maps_ref, rate_ref, skip_ref, *refs):
    finals, (own, other, fin, res) = refs[:ROW], refs[ROW:]
    core = lax.rem(lax.axis_index("tp"), 2)
    y = lax.rem(lax.axis_index("seq"), ROW)
    for o in range(ROW):
        fin[lax.rem(y + ROW - o, ROW)] = finals[o][STATE_ROWS:, :]
    maps = maps_ref[0].astype(F32)
    eye = lax.broadcasted_iota(jnp.int32, (NS, NS), 0) == lax.broadcasted_iota(jnp.int32, (NS, NS), 1)

    def column(k, at):
        return jnp.sum(jnp.where(eye, maps[k : k + 1, at : at + NS], 0.0), axis=1, keepdims=True)

    b_cols = [column(k, 0) for k in range(4)]
    c_cols = [column(k, NS) for k in range(4)]
    heads = WC // HP
    rows = lax.broadcasted_iota(jnp.int32, (heads, WC), 0)
    cols = lax.broadcasted_iota(jnp.int32, (heads, WC), 1)
    spread = jnp.where(rows == (cols >> 6), 1.0, 0.0).astype(F32)
    raw = [inputs[t, DEC_X + 32 : DEC_X + 48, :].astype(F32)[:4, :heads] for t in range(TP)]
    step = softplus(jnp.concatenate(raw, axis=0))
    parts = [slice(t * heads, (t + 1) * heads) for t in range(TP)]
    rates = jnp.concatenate([jnp.broadcast_to(rate_ref[:, part], (4, heads)) for part in parts], axis=0)
    skips = jnp.concatenate([skip_ref[:, part] for part in parts], axis=0)
    small = jnp.concatenate([step, jnp.exp(-step * rates), skips], axis=0)
    wide = jnp.dot(small, spread, precision=highest, preferred_element_type=F32)

    def unfold(rows):
        return jnp.concatenate([rows[q * 4 : (q + 1) * 4] for q in range(4)], axis=1)

    sums = [jnp.zeros((1, 1), F32)] * 4
    for t in range(TP):
        x = unfold(inputs[t, DEC_X : DEC_X + 16, :].astype(F32))
        z = unfold(inputs[t, DEC_X + 16 : DEC_X + 32, :].astype(F32))
        gate = z / (1.0 + jnp.exp(-z))
        chunks = [t * CHUNKS + i for i in range(CHUNKS)]
        state = jnp.concatenate(
            [fin[k // PARTS, k % PARTS * NS : (k % PARTS + 1) * NS, :].astype(F32) for k in chunks], axis=1
        )
        skip = wide[8 * TP + t : 8 * TP + t + 1]
        for k in range(4):
            wide_step = wide[4 * t + k : 4 * t + k + 1]
            fade = wide[4 * TP + 4 * t + k : 4 * TP + 4 * t + k + 1]
            state = fade * state + b_cols[k] * (wide_step * x[k : k + 1])
            read = jnp.sum(c_cols[k] * state, axis=0, keepdims=True) + skip * x[k : k + 1]
            v = read * gate[k : k + 1]
            res[t, NS + k : NS + k + 1, :] = v
            sums[k] = sums[k] + jnp.sum(v * v, axis=1, keepdims=True)
        res[t, :NS, :] = state
    factor = jnp.concatenate([lax.rsqrt(sums[k] / WIDTH + 1e-05) for k in range(4)], axis=0)
    for t in range(TP):
        res[t, NS : NS + 4, :] = res[t, NS : NS + 4, :] * factor
        res[t, NS + 4 :, :] = jnp.zeros((4, WC), F32)
    for z in range(ROW):
        own[z] = res[2 * z + core]
        other[z] = res[2 * z + 1 - core]


def decode(inputs, maps, rate, skip, finals):
    return pl.pallas_call(
        decode_kernel,
        out_shape=[jax.ShapeDtypeStruct((ROW, NS + 8, WC), F32)] * 2,
        in_specs=[VM] * (4 + ROW),
        out_specs=[VM] * 2,
        scratch_shapes=[
            pltpu.VMEM((ROW, FINAL_ROWS, LANE), BF16),
            pltpu.VMEM((TP, NS + 8, WC), F32),
        ],
        cost_estimate=cost(4),
        compiler_params=params(),
        name="decode",
    )(inputs, maps, rate, skip, *finals)


def side_kernel(group_ref, own, other, *outs):
    me = lax.axis_index("tp")
    z, core = lax.div(me, 2), lax.rem(me, 2)
    mine = lax.rem(lax.div(my_prompt(group_ref), 2), 2) == core
    for o in range(ROW):
        at = lax.rem(z + o, ROW)
        outs[o][...] = jnp.where(mine, own[at], other[at])


def choose_side(group_of, own, other):
    return pl.pallas_call(
        side_kernel,
        out_shape=[jax.ShapeDtypeStruct((NS + 8, WC), F32)] * ROW,
        in_specs=[SM, VM, VM],
        out_specs=[VM] * ROW,
        cost_estimate=cost(1),
        compiler_params=params(),
        name="choose_side",
    )(group_of, own, other)


def along_z(arrays):
    moves = [[(i, (i + 2 * o) % TP) for i in range(TP)] for o in range(ROW)]
    return [arrays[0]] + [lax.ppermute(arrays[o], "tp", moves[o]) for o in range(1, ROW)]


def along_y(arrays):
    moves = [[(x * ROW + y, x * ROW + (y + o) % ROW) for x in range(ROW) for y in range(ROW)] for o in range(ROW)]
    return [arrays[0]] + [lax.ppermute(arrays[o], "seq", moves[o]) for o in range(1, ROW)]


def shards(
    x_in, dt_raw, bc_in, decay_rate, skip_gain, kv_pre, lengths, group_of, slot_of,
    dec_x, dec_dt, dec_bc, dec_z, norm_gain, dec_q, dec_kv,
):
    rate = decay_rate.reshape(1, HEADS)
    skip = skip_gain.reshape(1, HEADS)
    gain = norm_gain.reshape(1, -1)
    maps = jnp.swapaxes(bc_in, 1, 2)
    table = jnp.concatenate([group_of, lengths, slot_of.reshape(-1)])

    *local, sent = local_states(lengths, x_in, dt_raw, maps, rate, kv_pre, dec_x, dec_z, dec_dt)
    pages = lax.all_to_all(sent, "tp", split_axis=0, concat_axis=0, tiled=True)
    blocks = along_y(local)
    own = row_totals(blocks)
    near = lax.ppermute(own, "seq", [(i, i ^ ROW) for i in range(SEQ)])
    across = [(x * ROW + y, (ROW - 1 - x) * ROW + y) for x in range(ROW) for y in range(ROW)]
    far = lax.ppermute(pair_totals(own, near), "seq", across)
    pages, unused = lax.optimization_barrier((pages, far))
    entering = along_y(enter_states(group_of, own, near, far, blocks))
    ordered, entering = lax.optimization_barrier((order_pages(group_of, pages), entering))
    recv = lax.all_to_all(ordered, "seq", split_axis=0, concat_axis=0, tiled=True)
    own, other = decode(pages, dec_bc, rate, skip, entering)
    other = lax.ppermute(other, "tp", [(i, i ^ 1) for i in range(TP)])
    results = along_z(choose_side(group_of, own, other))
    y_pre = block_outputs(lengths, x_in, dt_raw, maps, rate, skip, entering)
    kv_pool, dec_attn, dec_state, dec_mamba = attend(
        table, recv, dec_q, dec_kv, gain, results
    )
    return (y_pre, kv_pool, dec_mamba, dec_state, dec_attn)


def solution(mesh):
    return jax.shard_map(
        shards,
        mesh=mesh,
        in_specs=(
            P("tp", "seq", None),
            P("tp", "seq", None),
            P("tp", "seq", None),
            P(),
            P(),
            P("tp", "seq", None),
            P(),
            P(),
            P(),
            P("seq", None, "tp"),
            P("seq", None, "tp"),
            P("seq", None, None),
            P("seq", None, "tp"),
            P("tp"),
            P("seq", None, "tp"),
            P("seq", None, "tp"),
        ),
        out_specs=(
            P("tp", "seq", None),
            P("seq", None, "tp"),
            P("seq", None, "tp"),
            P("seq", None, "tp"),
            P("seq", None, "tp"),
        ),
        check_vma=False,
    )
```
